1024 devices in a mesh: dp: 4 (over x), expert: 32 (over z), seq: 8 (over y, core).
Axes of the slice: x: 4, y: 4, z: 32, core: 2. Of those that a mesh axis runs over, the one named last changes fastest.
Arguments:
- tokens: bfloat16 [131072, 1024], P(('dp', 'expert', 'seq')), parts along dimension 0, may hold values from -6 to 6
- picks: int32 [1024, 32, 16], P(('dp', 'expert', 'seq')), parts along dimension 0, may hold values from 0 to 127, as said below
- gates: float32 [1024, 32, 16], P(('dp', 'expert', 'seq')), parts along dimension 0, may hold values from 0.1 to 2
- counts: int32 [1024, 32], P(('dp', 'expert', 'seq')), parts along dimension 0, may hold values from 1 to 16, as said below
- norm_in: float32 [1024], replicated, may hold values from 0.1 to 1.9
- norm_out: float32 [1024], replicated, may hold values from 0.1 to 1.9
- w_in: bfloat16 [32, 1024, 1408], P('expert'), may hold values from -0.1875 to 0.1875
- w_out: bfloat16 [32, 1408, 1024], P('expert'), may hold values from -0.15625 to 0.15625
- w_key: bfloat16 [1024, 512], replicated, may hold values from -0.1875 to 0.1875
- w_value: bfloat16 [1024, 512], replicated, may hold values from -0.1875 to 0.1875
- queries: bfloat16 [32768, 512], P(('dp', 'expert', 'seq')), parts along dimension 0, may hold values from -300 to 300
- w_proj: bfloat16 [512, 1024], replicated, may hold values from -0.25 to 0.25
Outputs:
- encoded: bfloat16 [131072, 1024], P(('dp', 'expert', 'seq')), parts along dimension 0
- dec_out: bfloat16 [32768, 1024], P(('dp', 'expert', 'seq')), parts along dimension 0
The draws below stay inside these ranges and needn't reach their ends.
There are 4 independent parts, one for each index of `dp`. The reference program is written for one: setup_inputs(seed, part) draws one part's arguments, and reference() takes and returns one part's arrays. A program takes and returns all parts, laid end to end along the dimension named above; an argument that names none is the same for every part. Nothing has to cross between parts.
Inputs may be any that keep to these rules, and one draw needn't show every extreme that they name: `picks`: for each source device and expert, 16 different row numbers of that device's 128 tokens. Slots c < counts are live, the rest are padding; some source device and expert has all 16 slots live.
All inputs are finite; a program needn't handle non-finite values.
Results may differ from the reference program's by a relative error of at most 0.015.
The reference program's roundings to bfloat16 on the way count: a program that leaves them out, or rounds other values in their place, can miss the bound.
Values may be sent and summed in bfloat16 or wider, within the bound.
No kernel may reach another device: no remote copies, remote signals or barrier semaphores. Data moves between devices by JAX's collectives and lax.ppermute only.
A program may use at most 32 MiB of HBM per device.

```python
import math
import jax
import jax.numpy as jnp
from jax import lax

D = 1024
FF = 1408
HEADS = 8
TOK_DEV = 128
DEC_DEV = 32
EXPERTS = 32
CAP = 16
SOURCES = 256
TOKENS = 32768
DEC_TOKENS = 8192
HQ = 512
N_EXPERT = 32
N_SEQ = 8


def draw_picks(key, part):
    subkeys = jax.random.split(jax.random.fold_in(key, 11), SOURCES * EXPERTS)

    def choose(subkey):
        return jax.random.permutation(subkey, TOK_DEV)[:CAP]
    chosen = jax.vmap(choose)(subkeys)
    return chosen.reshape(SOURCES, EXPERTS, CAP).astype(jnp.int32)


def draw_counts(key, part):
    first, second = jax.random.split(jax.random.fold_in(key, 23))
    drawn = jax.random.randint(first, (SOURCES * EXPERTS,), 1, CAP + 1, dtype=jnp.int32)
    position = jax.random.randint(second, (), 0, SOURCES * EXPERTS, dtype=jnp.int32)
    drawn = drawn.at[position].set(CAP)
    return drawn.reshape(SOURCES, EXPERTS).astype(jnp.int32)


def draw_queries(key, part):
    first = jax.random.fold_in(jax.random.fold_in(key, 37), 0)
    base = jnp.clip(jax.random.normal(first, (DEC_TOKENS, HQ), jnp.float32), -6.0, 6.0)
    return base.astype(jnp.bfloat16)


def levels(own_key, dims, pieces, low, largest):
    level, own = 1.0, jax.random.fold_in(own_key, 6)
    for dim, blocks in pieces:
        heights = jnp.exp(jax.random.uniform(jax.random.fold_in(own, dim), (blocks,), jnp.float32, low / len(pieces), largest / len(pieces)))
        level = level * jnp.repeat(heights, dims[dim] // blocks).reshape([-1 if axis == dim else 1 for axis in range(len(dims))])
    return level


def scatter_about(own_key, dims, scale, bound, shards=(), kind=jnp.bfloat16):
    array = jax.random.normal(own_key, dims, jnp.float32) * scale
    if len(shards) > 0:
        array = levels(own_key, dims, shards, -0.22, 0.18) * array
    return jnp.clip(array, min=-bound, max=bound).astype(kind)


def setup_inputs(seed: int = 0, part: int = 0) -> dict:
    key_of = jax.random.split(jax.random.key(seed), 13)
    part_splits = jax.random.split(jax.random.fold_in(key_of[12], part), 13)
    return {
        "tokens": scatter_about(part_splits[0], (TOKENS, D), 1.0, 6.0, ((0, 256),)),
        "picks": draw_picks(jax.random.fold_in(jax.random.fold_in(key_of[12], part), 71), part),
        "gates": jnp.clip(jnp.exp(math.log(2.0) - 2.9957323 * jax.random.uniform(part_splits[2], (SOURCES, EXPERTS, CAP), jnp.float32) ** levels(part_splits[2], (SOURCES, EXPERTS, CAP), ((0, 256),), -0.2, 0.2)), 0.1, 2.0),
        "counts": draw_counts(jax.random.fold_in(jax.random.fold_in(key_of[12], part), 71), part),
        "norm_in": jnp.clip(1.0 + 0.18 * jax.random.normal(key_of[4], (D,), jnp.float32), 0.1, 1.9),
        "norm_out": jnp.clip(1.0 + 0.18 * jax.random.normal(key_of[5], (D,), jnp.float32), 0.1, 1.9),
        "w_in": scatter_about(key_of[6], (EXPERTS, D, FF), D ** -0.5, 0.1875, ((0, 32),)),
        "w_out": scatter_about(key_of[7], (EXPERTS, FF, D), FF ** -0.5, 0.15625, ((0, 32),)),
        "w_key": scatter_about(key_of[8], (D, HQ), D ** -0.5, 0.1875),
        "w_value": scatter_about(key_of[9], (D, HQ), D ** -0.5, 0.1875),
        "queries": draw_queries(jax.random.fold_in(jax.random.fold_in(key_of[12], part), 71), part),
        "w_proj": scatter_about(key_of[11], (HQ, D), HQ ** -0.5, 0.25),
    }


EPSILON = 1e-06

def rms_norm(values, gain):
    mean_square = lax.optimization_barrier(jnp.mean(values * values, axis=-1, keepdims=True))
    return values * lax.rsqrt(mean_square + EPSILON) * gain

def reference(tokens, picks, gates, counts, norm_in, norm_out, w_in, w_out, w_key, w_value, queries, w_proj):
    model_width = tokens.shape[1]
    plain = tokens.astype(jnp.float32)
    normed = rms_norm(plain, norm_in.astype(jnp.float32)).astype(jnp.bfloat16)
    offsets = jnp.arange(SOURCES, dtype=jnp.int32) * TOK_DEV
    row_index = (picks + offsets[:, None, None]).astype(jnp.int32)

    def expert_apply(expert):
        chosen = jnp.take(normed, row_index[:, expert, :].reshape(-1), axis=0)
        hidden = jax.nn.gelu(jnp.dot(chosen, w_in[expert], preferred_element_type=jnp.float32), approximate=True).astype(jnp.bfloat16)
        return jnp.dot(hidden, w_out[expert], preferred_element_type=jnp.float32).astype(jnp.bfloat16)
    outputs = lax.map(expert_apply, jnp.arange(EXPERTS, dtype=jnp.int32))
    ordered = outputs.reshape(EXPERTS, SOURCES, CAP, model_width).transpose(1, 0, 2, 3)
    live = (jnp.arange(CAP, dtype=jnp.int32)[None, None, :] < counts[:, :, None]).astype(jnp.float32)
    slot_weight = gates.astype(jnp.float32) * live
    terms = ordered.astype(jnp.float32) * slot_weight[..., None]
    expert_sum = jnp.zeros((TOKENS, model_width), jnp.float32).at[row_index.reshape(-1)].add(terms.reshape(-1, model_width))
    mixed = plain + expert_sum
    encoded = rms_norm(mixed, norm_out.astype(jnp.float32)).astype(jnp.bfloat16)
    key_proj = jnp.dot(encoded, w_key, preferred_element_type=jnp.float32).astype(jnp.bfloat16)
    value_proj = jnp.dot(encoded, w_value, preferred_element_type=jnp.float32).astype(jnp.bfloat16)
    head_size = queries.shape[1] // HEADS
    seq_length = N_SEQ * TOK_DEV
    key_heads = key_proj.reshape(N_EXPERT, seq_length, HEADS, head_size)
    value_heads = value_proj.reshape(N_EXPERT, seq_length, HEADS, head_size)
    query_heads = queries.reshape(N_EXPERT, N_SEQ * DEC_DEV, HEADS, head_size)

    def attend(inputs):
        query_block, key_block, value_block = inputs
        scores = jnp.einsum('qhd,khd->qhk', query_block.astype(jnp.float32), key_block.astype(jnp.float32)) * head_size ** (-0.5)
        row_max = lax.optimization_barrier(jnp.max(scores, axis=-1, keepdims=True))
        weights = jnp.exp(scores - row_max)
        row_total = lax.optimization_barrier(jnp.sum(weights, axis=-1))
        rounded = lax.optimization_barrier(weights.astype(jnp.bfloat16)).astype(jnp.float32)
        context = jnp.einsum('qhk,khd->qhd', rounded, value_block.astype(jnp.float32)) / row_total[..., None]
        return context.astype(jnp.bfloat16)
    contexts = lax.map(attend, (query_heads, key_heads, value_heads))
    context = contexts.reshape(DEC_TOKENS, HEADS * head_size)
    dec_out = jnp.dot(context, w_proj, preferred_element_type=jnp.float32).astype(jnp.bfloat16)
    return (encoded, dec_out)
```

```python
import functools

import jax
import jax.numpy as jnp
from jax import lax
from jax.experimental import pallas as pl
from jax.experimental.pallas import tpu as pltpu
from jax.sharding import Mesh
from jax.sharding import PartitionSpec as P

HEADS = 8
EPSILON = 1e-06
BLOCK = 2
ALL = ("dp", "block", "parity", "row", "core")
NEAR = ("dp", "parity", "row", "core")
SEQ = ("row", "core")
STEP_J, STEP_E, INV_J = 9, 30, 25
STATS = 5
VMEM = 60 * 1024 * 1024
F32 = jnp.float32
BF16 = jnp.bfloat16

_VM = functools.partial(pl.BlockSpec, memory_space=pltpu.VMEM)


def rms_norm(values, gain):
    mean_square = jnp.mean(values * values, axis=-1, keepdims=True)
    return values * lax.rsqrt(mean_square + EPSILON) * gain


def shard_kernel(which, w_in_ref, w_out_ref, out_ref):
    rows = out_ref.shape[0]
    block, kind = which[0], which[1]

    @pl.when(kind == 0)
    def _():
        out_ref[...] = w_in_ref[0]

    @pl.when(kind == 1)
    def _():
        turned = w_out_ref[0].astype(F32).T
        upper = jnp.where(block % 2 == 1, turned[rows:], turned[:rows])
        out_ref[...] = upper.astype(BF16)


def take_shard(which, w_in, w_out, blocks):
    width, hidden = w_in.shape[1], w_in.shape[2]
    rows = width // blocks
    return pl.pallas_call(
        shard_kernel,
        grid_spec=pltpu.PrefetchScalarGridSpec(
            num_scalar_prefetch=1,
            grid=(1,),
            in_specs=[
                pl.BlockSpec((1, rows, hidden), lambda i, s: (0, s[0], 0)),
                pl.BlockSpec((1, hidden, 2 * rows), lambda i, s: (0, 0, s[0] // 2)),
            ],
            out_specs=pl.BlockSpec((rows, hidden), lambda i, s: (0, 0)),
        ),
        out_shape=jax.ShapeDtypeStruct((rows, hidden), BF16),
        compiler_params=pltpu.CompilerParams(vmem_limit_bytes=VMEM // 4),
    )(which, w_in, w_out)


def pick_kernel(tokens_ref, gain_ref, picks_ref, out_ref):
    rows = tokens_ref.shape[0]
    normed = rms_norm(tokens_ref[...].astype(F32), gain_ref[...]).astype(BF16)
    slots = picks_ref.shape[1]
    here = lax.broadcasted_iota(jnp.int32, (rows, slots), 0) == picks_ref[...]
    onehot = jnp.where(here, 1.0, 0.0).astype(BF16)
    out_ref[...] = lax.dot_general(
        onehot, normed, (((0,), (0,)), ((), ())), preferred_element_type=F32
    ).astype(BF16)


def pick_rows(tokens, gain, picks):
    slots, width = picks.shape[1], tokens.shape[1]
    return pl.pallas_call(
        pick_kernel,
        in_specs=[_VM()] * 3,
        out_specs=_VM(),
        out_shape=jax.ShapeDtypeStruct((slots, width), BF16),
        compiler_params=pltpu.CompilerParams(vmem_limit_bytes=VMEM // 4),
    )(tokens, gain, picks)


def gelu(v):
    return 0.5 * v * (1.0 + jnp.tanh(0.7978845608028654 * (v + 0.044715 * (v * v * v))))


def expert_kernel(rows_ref, weights_ref, out_ref, w_in, w_out, sems):
    first = pltpu.make_async_copy(weights_ref.at[:, 0], w_in, sems.at[0])
    second = pltpu.make_async_copy(weights_ref.at[:, 1], w_out, sems.at[1])
    first.start()
    second.start()
    first.wait()
    width, hidden = rows_ref.shape[1], w_in.shape[2]
    tile = 256
    second.wait()

    @pl.loop(0, rows_ref.shape[0] // tile)
    def _(i):
        here = pl.ds(pl.multiple_of(i * tile, tile), tile)
        mid = gelu(
            jnp.dot(
                rows_ref[here, :], w_in[...].reshape(width, hidden), preferred_element_type=F32
            )
        ).astype(BF16)
        out_ref[here, :] = lax.dot_general(
            mid,
            w_out[...].reshape(width, hidden),
            (((1,), (1,)), ((), ())),
            preferred_element_type=F32,
        ).astype(BF16)


def expert(rows, weights):
    total, width = rows.shape
    blocks, _, part, hidden = weights.shape
    return pl.pallas_call(
        expert_kernel,
        in_specs=[_VM(), pl.BlockSpec(memory_space=pl.ANY)],
        out_specs=_VM(),
        out_shape=jax.ShapeDtypeStruct((total, width), BF16),
        scratch_shapes=[
            pltpu.VMEM((blocks, part, hidden), BF16),
            pltpu.VMEM((blocks, part, hidden), BF16),
            pltpu.SemaphoreType.DMA((2,)),
        ],
        compiler_params=pltpu.CompilerParams(vmem_limit_bytes=VMEM // 2),
        cost_estimate=pl.CostEstimate(
            flops=4 * total * width * hidden,
            bytes_accessed=4 * width * hidden + 4 * total * width,
            transcendentals=total * hidden,
        ),
    )(rows, weights)


def pieces(v, count):
    out = []
    for _ in range(count):
        part = v.astype(BF16)
        out.append(part)
        v = v - part.astype(F32)
    return out


def tail_kernel(
    back_ref, picks_ref, weight_ref, tokens_ref, gain_ref, key_ref, value_ref, query_ref,
    encoded_ref, packet_ref,
):
    rows = tokens_ref.shape[0]
    slots = picks_ref.shape[1]
    here = lax.broadcasted_iota(jnp.int32, (rows, slots), 0) == picks_ref[...]
    spread = jnp.where(here, weight_ref[...], 0.0)
    back = back_ref[...]
    expert_sum = sum(
        jnp.dot(part, back, preferred_element_type=F32) for part in pieces(spread, 3)
    )
    mixed = tokens_ref[...].astype(F32) + expert_sum
    encoded = rms_norm(mixed, gain_ref[...]).astype(BF16)
    encoded_ref[...] = encoded
    keys = jnp.dot(encoded, key_ref[...], preferred_element_type=F32).astype(BF16)
    values = jnp.dot(encoded, value_ref[...], preferred_element_type=F32).astype(BF16)
    query = query_ref[...]
    count, features = query.shape
    size = features // HEADS
    lane = lax.broadcasted_iota(jnp.int32, (rows, 2 * size), 1)
    low = lane < size
    zero = jnp.zeros((), BF16)
    stat_lane = lax.broadcasted_iota(jnp.int32, (count, 128), 1)
    stats = jnp.zeros((count, 128), F32)
    for pair in range(HEADS // 2):
        span = slice(pair * 2 * size, (pair + 1) * 2 * size)
        q, k, v = query[:, span], keys[:, span], values[:, span]
        total = None
        for odd in range(2):
            mask = low if odd == 0 else ~low
            scores = lax.dot_general(
                q,
                jnp.where(mask, k, zero),
                (((1,), (1,)), ((), ())),
                preferred_element_type=F32,
            ) * (size**-0.5)
            top = jnp.max(scores, axis=1, keepdims=True)
            weights = jnp.exp(scores - top)
            amount = jnp.sum(weights, axis=1, keepdims=True)
            term = jnp.dot(
                weights.astype(BF16), jnp.where(mask, v, zero), preferred_element_type=F32
            )
            total = term if total is None else total + term
            entries = pieces(top, 3) + pieces(amount, 2)
            for i, entry in enumerate(entries):
                at = (2 * pair + odd) * STATS + i
                stats = jnp.where(stat_lane == at, entry.astype(F32), stats)
        packet_ref[:, span] = total.astype(BF16)
    packet_ref[:, features:] = stats.astype(BF16)


def tail(back, picks, weight, tokens, gain, w_key, w_value, query):
    rows, width = tokens.shape
    count, features = query.shape
    return pl.pallas_call(
        tail_kernel,
        in_specs=[_VM()] * 8,
        out_specs=(_VM(), _VM()),
        out_shape=(
            jax.ShapeDtypeStruct((rows, width), BF16),
            jax.ShapeDtypeStruct((count, features + 128), BF16),
        ),
        compiler_params=pltpu.CompilerParams(vmem_limit_bytes=VMEM // 2),
    )(back, picks, weight, tokens, gain, w_key, w_value, query)


def merge_kernel(got_ref, proj_ref, out_ref):
    group, count, wide = got_ref.shape
    features = wide - 128
    size = features // HEADS
    lane = lax.broadcasted_iota(jnp.int32, (count, 2 * size), 1)
    low = lane < size
    stats = [got_ref[g, :, features:].astype(F32) for g in range(group)]
    parts = []
    for pair in range(HEADS // 2):
        span = slice(pair * 2 * size, (pair + 1) * 2 * size)
        scales, totals = [], []
        for odd in range(2):
            at = (2 * pair + odd) * STATS
            tops = [s[:, at : at + 1] + s[:, at + 1 : at + 2] + s[:, at + 2 : at + 3] for s in stats]
            amounts = [s[:, at + 3 : at + 4] + s[:, at + 4 : at + 5] for s in stats]
            top = functools.reduce(jnp.maximum, tops)
            scale = [jnp.exp(t - top) for t in tops]
            scales.append(scale)
            totals.append(sum(a * s for a, s in zip(amounts, scale)))
        weighted = sum(
            got_ref[g, :, span].astype(F32) * jnp.where(low, scales[0][g], scales[1][g])
            for g in range(group)
        )
        parts.append((weighted / jnp.where(low, totals[0], totals[1])).astype(BF16))
    context = jnp.concatenate(parts, axis=1)
    out_ref[...] = jnp.dot(context, proj_ref[...], preferred_element_type=F32).astype(BF16)


def merge(got, w_proj):
    return pl.pallas_call(
        merge_kernel,
        in_specs=[_VM()] * 2,
        out_specs=_VM(),
        out_shape=jax.ShapeDtypeStruct((got.shape[1], w_proj.shape[1]), BF16),
        compiler_params=pltpu.CompilerParams(vmem_limit_bytes=VMEM // 4),
    )(got, w_proj)


def scatter_pairs(sizes):
    dps, blocks, parities, rows, cores = sizes
    plane = dps * rows * cores

    def place(dp, z, row, core):
        return ((dp * blocks * parities + z) * rows + row) * cores + core

    pairs = []
    for dp in range(dps):
        for parity in range(parities):
            for row in range(rows):
                e = (dp * parities + parity) * rows + row
                for block in range(blocks):
                    for core in range(cores):
                        j = block * cores + core
                        column = (STEP_J * j + STEP_E * e) % plane
                        source = place(
                            column // (rows * cores), e, column // cores % rows, column % cores
                        )
                        pairs.append((source, place(dp, block * parities + parity, row, core)))
    return pairs


def local(
    sizes, tokens, picks, gates, counts, norm_in, norm_out, w_in, w_out, w_key, w_value, queries, w_proj
):
    dps, blocks, parities, row_count, cores = sizes
    plane = dps * row_count * cores
    experts, cap = picks.shape[1], picks.shape[2]
    width = tokens.shape[1]
    own = lax.axis_index("block") * parities + lax.axis_index("parity")
    column = (lax.axis_index("dp") * row_count + lax.axis_index("row")) * cores + lax.axis_index(
        "core"
    )
    j = (INV_J * (column + (plane - STEP_E) * own)) % plane
    shard = take_shard(jnp.stack([j // cores, j % cores]).astype(jnp.int32), w_in, w_out, blocks)
    shard = lax.ppermute(shard, ALL, scatter_pairs(sizes))
    weights = lax.all_gather(shard, ("block", "core"))
    weights = weights.reshape(blocks, cores, *shard.shape)

    pick_row = picks.reshape(1, experts * cap)
    live = lax.broadcasted_iota(jnp.int32, (experts, cap), 1) < counts[0][:, None]
    slot_weight = jnp.where(live, gates[0], 0.0).reshape(1, experts * cap)
    chosen = pick_rows(tokens, norm_in[None, :], pick_row)
    near = experts * cores
    there = lax.all_to_all(
        chosen.reshape(near, -1, width), NEAR, split_axis=0, concat_axis=0, tiled=True
    )
    query = lax.all_gather(queries, SEQ, tiled=True)

    result = expert(there.reshape(-1, width), weights)
    back = lax.all_to_all(
        result.reshape(near, -1, width), NEAR, split_axis=0, concat_axis=0, tiled=True
    ).reshape(-1, width)
    encoded, packet = tail(
        back, pick_row, slot_weight, tokens, norm_out[None, :], w_key, w_value, query
    )
    group = row_count * cores
    got = lax.all_to_all(
        packet.reshape(group, -1, packet.shape[1]), SEQ, split_axis=0, concat_axis=0, tiled=True
    )
    return encoded, merge(got, w_proj)


def solution(mesh):
    dps, planes, seq = mesh.shape["dp"], mesh.shape["expert"], mesh.shape["seq"]
    sizes = (dps, planes // BLOCK, BLOCK, seq // 2, 2)
    split = Mesh(mesh.devices.reshape(sizes), ALL)
    in_specs = (
        P(ALL, None),
        P(ALL, None, None),
        P(ALL, None, None),
        P(ALL, None),
        P(),
        P(),
        P(("block", "parity"), None, None),
        P(("block", "parity"), None, None),
        P(),
        P(),
        P(ALL, None),
        P(),
    )
    out_specs = (P(ALL, None), P(ALL, None))
    return jax.shard_map(
        functools.partial(local, sizes),
        mesh=split,
        in_specs=in_specs,
        out_specs=out_specs,
        check_vma=False,
    )
```

```python
import functools

import jax
import jax.numpy as jnp
from jax import lax
from jax.experimental import pallas as pl
from jax.experimental.pallas import tpu as pltpu
from jax.sharding import Mesh
from jax.sharding import PartitionSpec as P

HEADS = 8
EPSILON = 1e-06
BLOCK = 2
ALL = ("dp", "block", "parity", "row", "core")
NEAR = ("dp", "parity", "row", "core")
SEQ = ("row", "core")
STEP_J, STEP_E, INV_J = 9, 30, 25
STATS = 5
VMEM = 60 * 1024 * 1024
FULL = 61 * 1024 * 1024
F32 = jnp.float32
BF16 = jnp.bfloat16

_VM = functools.partial(pl.BlockSpec, memory_space=pltpu.VMEM)


def rms_norm(values, gain):
    mean_square = jnp.mean(values * values, axis=-1, keepdims=True)
    return values * lax.rsqrt(mean_square + EPSILON) * gain


def shard_kernel(which, w_in_ref, w_out_ref, out_ref):
    rows = out_ref.shape[0]
    block, kind = which[0], which[1]

    @pl.when(kind == 0)
    def _():
        out_ref[...] = w_in_ref[0]

    @pl.when(kind == 1)
    def _():
        turned = w_out_ref[0].astype(F32).T
        upper = jnp.where(block % 2 == 1, turned[rows:], turned[:rows])
        out_ref[...] = upper.astype(BF16)


def take_shard(which, w_in, w_out, blocks):
    width, hidden = w_in.shape[1], w_in.shape[2]
    rows = width // blocks
    return pl.pallas_call(
        shard_kernel,
        grid_spec=pltpu.PrefetchScalarGridSpec(
            num_scalar_prefetch=1,
            grid=(1,),
            in_specs=[
                pl.BlockSpec((1, rows, hidden), lambda i, s: (0, s[0], 0)),
                pl.BlockSpec((1, hidden, 2 * rows), lambda i, s: (0, 0, s[0] // 2)),
            ],
            out_specs=pl.BlockSpec((rows, hidden), lambda i, s: (0, 0)),
        ),
        out_shape=jax.ShapeDtypeStruct((rows, hidden), BF16),
        compiler_params=pltpu.CompilerParams(vmem_limit_bytes=FULL),
    )(which, w_in, w_out)


def pick_kernel(tokens_ref, gain_ref, picks_ref, out_ref):
    rows = tokens_ref.shape[0]
    normed = rms_norm(tokens_ref[...].astype(F32), gain_ref[...]).astype(BF16)
    slots = picks_ref.shape[1]
    here = lax.broadcasted_iota(jnp.int32, (rows, slots), 0) == picks_ref[...]
    onehot = jnp.where(here, 1.0, 0.0).astype(BF16)
    out_ref[...] = lax.dot_general(
        onehot, normed, (((0,), (0,)), ((), ())), preferred_element_type=F32
    ).astype(BF16)


def pick_rows(tokens, gain, picks):
    slots, width = picks.shape[1], tokens.shape[1]
    return pl.pallas_call(
        pick_kernel,
        in_specs=[_VM()] * 3,
        out_specs=_VM(),
        out_shape=jax.ShapeDtypeStruct((slots, width), BF16),
        compiler_params=pltpu.CompilerParams(vmem_limit_bytes=VMEM // 4),
    )(tokens, gain, picks)


def gelu(v):
    return 0.5 * v * (1.0 + jnp.tanh(0.7978845608028654 * (v + 0.044715 * (v * v * v))))


def expert_kernel(place, rows_ref, gathered_ref, own_ref, *refs):
    blocks = gathered_ref.shape[0]
    ring = refs[:-7]
    early, late, out_ref, w_in, w_out, middle, sems = refs[-7:]
    block, turn = place[0], place[1]
    head = gathered_ref.shape[2]
    rest = pl.ds(head, own_ref.shape[0] // 2)

    def at(offset):
        return lax.rem(block + offset + blocks, blocks)

    def halves(ref, start, index):
        size = own_ref.shape[0] // 2
        return [
            (ref.at[pl.ds(start + k * size, size)], buffer.at[index, rest])
            for k, buffer in enumerate((w_in, w_out))
        ]

    jobs = [
        [(gathered_ref.at[:, k], buffer.at[:, pl.ds(0, head)])]
        for k, buffer in enumerate((w_in, w_out))
    ]
    found = [halves(own_ref, 0, block)]
    for step, ref in enumerate(ring, 1):
        found.append(halves(ref, 0, at(-step * turn)))
    count = early.shape[0] // own_ref.shape[0]
    for step in range(1, len(ring)):
        ref, k = (early, step - 1) if step <= count else (late, step - 1 - count)
        found.append(halves(ref, k * own_ref.shape[0], at(step * turn)))
    for pair in found:
        for k in range(2):
            jobs[k].append(pair[k])
    copies = [
        [pltpu.make_async_copy(src, dst, sems.at[k, n]) for n, (src, dst) in enumerate(jobs[k])]
        for k in range(2)
    ]
    for part in copies:
        for copy in part:
            copy.start()
    width, hidden = rows_ref.shape[1], w_in.shape[2]
    tile = 256
    for copy in copies[0]:
        copy.wait()

    @pl.loop(0, rows_ref.shape[0] // tile)
    def _(i):
        here = pl.ds(pl.multiple_of(i * tile, tile), tile)
        middle[here, :] = gelu(
            jnp.dot(
                rows_ref[here, :], w_in[...].reshape(width, hidden), preferred_element_type=F32
            )
        ).astype(BF16)

    for copy in copies[1]:
        copy.wait()

    @pl.loop(0, rows_ref.shape[0] // tile)
    def _(i):
        here = pl.ds(pl.multiple_of(i * tile, tile), tile)
        out_ref[here, :] = lax.dot_general(
            middle[here, :],
            w_out[...].reshape(width, hidden),
            (((1,), (1,)), ((), ())),
            preferred_element_type=F32,
        ).astype(BF16)


def expert(place, rows, gathered, own, ring, early, late):
    total, width = rows.shape
    blocks, _, head, hidden = gathered.shape
    part = head + own.shape[0] // 2
    anywhere = pl.BlockSpec(memory_space=pl.ANY)
    return pl.pallas_call(
        expert_kernel,
        in_specs=[pl.BlockSpec(memory_space=pltpu.SMEM), _VM()]
        + [anywhere] * (4 + len(ring)),
        out_specs=_VM(),
        out_shape=jax.ShapeDtypeStruct((total, width), BF16),
        scratch_shapes=[
            pltpu.VMEM((blocks, part, hidden), BF16),
            pltpu.VMEM((blocks, part, hidden), BF16),
            pltpu.VMEM((total, hidden), BF16),
            pltpu.SemaphoreType.DMA((2, 1 + 2 * len(ring))),
        ],
        compiler_params=pltpu.CompilerParams(vmem_limit_bytes=FULL),
        cost_estimate=pl.CostEstimate(
            flops=4 * total * width * hidden,
            bytes_accessed=4 * width * hidden + 4 * total * width,
            transcendentals=total * hidden,
        ),
    )(place, rows, gathered, own, *ring, early, late)


def spread(shard, sizes):
    _, blocks, _, _, cores = sizes
    half = shard.shape[0] // 2
    gathered = lax.all_gather(shard[:half], ("block", "core"))
    gathered = gathered.reshape(blocks, cores, half, shard.shape[1])
    swap = [(0, 1), (1, 0)]
    core = lax.axis_index("core")
    mine = shard[half:]
    other = lax.ppermute(mine, "core", swap)
    own = jnp.where(
        core == 0, jnp.concatenate([mine, other]), jnp.concatenate([other, mine])
    )
    turns = [
        (b * cores + c, (b + (1 if c == 0 else -1)) % blocks * cores + c)
        for b in range(blocks)
        for c in range(cores)
    ]
    steps = blocks // 2
    ring, held = [], own
    for _ in range(steps):
        held = lax.ppermute(held, ("block", "core"), turns)
        ring.append(held)
    cut = steps // 2
    early = lax.ppermute(jnp.concatenate(ring[:cut]), "core", swap)
    late = lax.ppermute(jnp.concatenate(ring[cut : steps - 1]), "core", swap)
    place = jnp.stack([lax.axis_index("block"), 1 - 2 * core]).astype(jnp.int32)
    return place, gathered, own, ring, early, late


def pieces(v, count):
    out = []
    for _ in range(count):
        part = v.astype(BF16)
        out.append(part)
        v = v - part.astype(F32)
    return out


def tail_kernel(
    back_ref, picks_ref, weight_ref, tokens_ref, gain_ref, key_ref, value_ref, query_ref,
    encoded_ref, packet_ref,
):
    rows = tokens_ref.shape[0]
    slots = picks_ref.shape[1]
    here = lax.broadcasted_iota(jnp.int32, (rows, slots), 0) == picks_ref[...]
    spread = jnp.where(here, weight_ref[...], 0.0)
    back = back_ref[...]
    expert_sum = sum(
        jnp.dot(part, back, preferred_element_type=F32) for part in pieces(spread, 3)
    )
    mixed = tokens_ref[...].astype(F32) + expert_sum
    encoded = rms_norm(mixed, gain_ref[...]).astype(BF16)
    encoded_ref[...] = encoded
    keys = jnp.dot(encoded, key_ref[...], preferred_element_type=F32).astype(BF16)
    values = jnp.dot(encoded, value_ref[...], preferred_element_type=F32).astype(BF16)
    query = query_ref[...]
    count, features = query.shape
    size = features // HEADS
    lane = lax.broadcasted_iota(jnp.int32, (rows, 2 * size), 1)
    low = lane < size
    zero = jnp.zeros((), BF16)
    stat_lane = lax.broadcasted_iota(jnp.int32, (count, 128), 1)
    stats = jnp.zeros((count, 128), F32)
    for pair in range(HEADS // 2):
        span = slice(pair * 2 * size, (pair + 1) * 2 * size)
        q, k, v = query[:, span], keys[:, span], values[:, span]
        total = None
        for odd in range(2):
            mask = low if odd == 0 else ~low
            scores = lax.dot_general(
                q,
                jnp.where(mask, k, zero),
                (((1,), (1,)), ((), ())),
                preferred_element_type=F32,
            ) * (size**-0.5)
            top = jnp.max(scores, axis=1, keepdims=True)
            weights = jnp.exp(scores - top)
            amount = jnp.sum(weights, axis=1, keepdims=True)
            term = jnp.dot(
                weights.astype(BF16), jnp.where(mask, v, zero), preferred_element_type=F32
            )
            total = term if total is None else total + term
            entries = pieces(top, 3) + pieces(amount, 2)
            for i, entry in enumerate(entries):
                at = (2 * pair + odd) * STATS + i
                stats = jnp.where(stat_lane == at, entry.astype(F32), stats)
        packet_ref[:, span] = total.astype(BF16)
    packet_ref[:, features:] = stats.astype(BF16)


def tail(back, picks, weight, tokens, gain, w_key, w_value, query):
    rows, width = tokens.shape
    count, features = query.shape
    return pl.pallas_call(
        tail_kernel,
        in_specs=[_VM()] * 8,
        out_specs=(_VM(), _VM()),
        out_shape=(
            jax.ShapeDtypeStruct((rows, width), BF16),
            jax.ShapeDtypeStruct((count, features + 128), BF16),
        ),
        compiler_params=pltpu.CompilerParams(vmem_limit_bytes=VMEM // 2),
    )(back, picks, weight, tokens, gain, w_key, w_value, query)


def merge_kernel(got_ref, proj_ref, out_ref):
    group, count, wide = got_ref.shape
    features = wide - 128
    size = features // HEADS
    lane = lax.broadcasted_iota(jnp.int32, (count, 2 * size), 1)
    low = lane < size
    stats = [got_ref[g, :, features:].astype(F32) for g in range(group)]
    parts = []
    for pair in range(HEADS // 2):
        span = slice(pair * 2 * size, (pair + 1) * 2 * size)
        scales, totals = [], []
        for odd in range(2):
            at = (2 * pair + odd) * STATS
            tops = [s[:, at : at + 1] + s[:, at + 1 : at + 2] + s[:, at + 2 : at + 3] for s in stats]
            amounts = [s[:, at + 3 : at + 4] + s[:, at + 4 : at + 5] for s in stats]
            top = functools.reduce(jnp.maximum, tops)
            scale = [jnp.exp(t - top) for t in tops]
            scales.append(scale)
            totals.append(sum(a * s for a, s in zip(amounts, scale)))
        weighted = sum(
            got_ref[g, :, span].astype(F32) * jnp.where(low, scales[0][g], scales[1][g])
            for g in range(group)
        )
        parts.append((weighted / jnp.where(low, totals[0], totals[1])).astype(BF16))
    context = jnp.concatenate(parts, axis=1)
    out_ref[...] = jnp.dot(context, proj_ref[...], preferred_element_type=F32).astype(BF16)


def merge(got, w_proj):
    return pl.pallas_call(
        merge_kernel,
        in_specs=[_VM()] * 2,
        out_specs=_VM(),
        out_shape=jax.ShapeDtypeStruct((got.shape[1], w_proj.shape[1]), BF16),
        compiler_params=pltpu.CompilerParams(vmem_limit_bytes=VMEM // 4),
    )(got, w_proj)


def scatter_pairs(sizes):
    dps, blocks, parities, rows, cores = sizes
    plane = dps * rows * cores

    def place(dp, z, row, core):
        return ((dp * blocks * parities + z) * rows + row) * cores + core

    pairs = []
    for dp in range(dps):
        for parity in range(parities):
            for row in range(rows):
                e = (dp * parities + parity) * rows + row
                for block in range(blocks):
                    for core in range(cores):
                        j = block * cores + core
                        column = (STEP_J * j + STEP_E * e) % plane
                        source = place(
                            column // (rows * cores), e, column // cores % rows, column % cores
                        )
                        pairs.append((source, place(dp, block * parities + parity, row, core)))
    return pairs


def local(
    sizes, tokens, picks, gates, counts, norm_in, norm_out, w_in, w_out, w_key, w_value, queries, w_proj
):
    dps, blocks, parities, row_count, cores = sizes
    plane = dps * row_count * cores
    experts, cap = picks.shape[1], picks.shape[2]
    width = tokens.shape[1]
    own = lax.axis_index("block") * parities + lax.axis_index("parity")
    column = (lax.axis_index("dp") * row_count + lax.axis_index("row")) * cores + lax.axis_index(
        "core"
    )
    j = (INV_J * (column + (plane - STEP_E) * own)) % plane
    shard = take_shard(jnp.stack([j // cores, j % cores]).astype(jnp.int32), w_in, w_out, blocks)
    shard, picks = lax.optimization_barrier((shard, picks))
    shard = lax.ppermute(shard, ALL, scatter_pairs(sizes))
    weights = spread(shard, sizes)

    pick_row = picks.reshape(1, experts * cap)
    live = lax.broadcasted_iota(jnp.int32, (experts, cap), 1) < counts[0][:, None]
    slot_weight = jnp.where(live, gates[0], 0.0).reshape(1, experts * cap)
    chosen = pick_rows(tokens, norm_in[None, :], pick_row)
    near = experts * cores
    there = lax.all_to_all(
        chosen.reshape(near, -1, width), NEAR, split_axis=0, concat_axis=0, tiled=True
    )
    query = lax.all_gather(queries, SEQ, tiled=True)
    there, query = lax.optimization_barrier((there, query))

    place, gathered, own_part, ring, early, late = weights
    result = expert(place, there.reshape(-1, width), gathered, own_part, ring, early, late)
    back = lax.all_to_all(
        result.reshape(near, -1, width), NEAR, split_axis=0, concat_axis=0, tiled=True
    ).reshape(-1, width)
    encoded, packet = tail(
        back, pick_row, slot_weight, tokens, norm_out[None, :], w_key, w_value, query
    )
    group = row_count * cores
    got = lax.all_to_all(
        packet.reshape(group, -1, packet.shape[1]), SEQ, split_axis=0, concat_axis=0, tiled=True
    )
    return encoded, merge(got, w_proj)


def solution(mesh):
    dps, planes, seq = mesh.shape["dp"], mesh.shape["expert"], mesh.shape["seq"]
    sizes = (dps, planes // BLOCK, BLOCK, seq // 2, 2)
    split = Mesh(mesh.devices.reshape(sizes), ALL)
    in_specs = (
        P(ALL, None),
        P(ALL, None, None),
        P(ALL, None, None),
        P(ALL, None),
        P(),
        P(),
        P(("block", "parity"), None, None),
        P(("block", "parity"), None, None),
        P(),
        P(),
        P(ALL, None),
        P(),
    )
    out_specs = (P(ALL, None), P(ALL, None))
    return jax.shard_map(
        functools.partial(local, sizes),
        mesh=split,
        in_specs=in_specs,
        out_specs=out_specs,
        check_vma=False,
    )
```

```python
import functools

import jax
import jax.numpy as jnp
from jax import lax
from jax.experimental import pallas as pl
from jax.experimental.pallas import tpu as pltpu
from jax.sharding import Mesh
from jax.sharding import PartitionSpec as P

HEADS = 8
EPSILON = 1e-06
BLOCK = 2
ALL = ("dp", "block", "parity", "row", "core")
NEAR = ("dp", "parity", "row", "core")
SEQ = ("row", "core")
STEP_J, STEP_E, INV_J = 9, 30, 25
STATS = 5
VMEM = 60 * 1024 * 1024
FULL = 61 * 1024 * 1024
F32 = jnp.float32
BF16 = jnp.bfloat16

_VM = functools.partial(pl.BlockSpec, memory_space=pltpu.VMEM)


def rms_norm(values, gain):
    mean_square = jnp.mean(values * values, axis=-1, keepdims=True)
    return values * lax.rsqrt(mean_square + EPSILON) * gain


def shard_kernel(which, w_in_ref, w_out_ref, out_ref):
    rows = out_ref.shape[0]
    block, kind = which[0], which[1]

    @pl.when(kind == 0)
    def _():
        out_ref[...] = w_in_ref[0]

    @pl.when(kind == 1)
    def _():
        turned = w_out_ref[0].astype(F32).T
        upper = jnp.where(block % 2 == 1, turned[rows:], turned[:rows])
        out_ref[...] = upper.astype(BF16)


def take_shard(which, w_in, w_out, blocks):
    width, hidden = w_in.shape[1], w_in.shape[2]
    rows = width // blocks
    return pl.pallas_call(
        shard_kernel,
        grid_spec=pltpu.PrefetchScalarGridSpec(
            num_scalar_prefetch=1,
            grid=(1,),
            in_specs=[
                pl.BlockSpec((1, rows, hidden), lambda i, s: (0, s[0], 0)),
                pl.BlockSpec((1, hidden, 2 * rows), lambda i, s: (0, 0, s[0] // 2)),
            ],
            out_specs=pl.BlockSpec((rows, hidden), lambda i, s: (0, 0)),
        ),
        out_shape=jax.ShapeDtypeStruct((rows, hidden), BF16),
        compiler_params=pltpu.CompilerParams(vmem_limit_bytes=FULL),
    )(which, w_in, w_out)


def pick_kernel(tokens_ref, gain_ref, picks_ref, out_ref):
    rows = tokens_ref.shape[0]
    normed = rms_norm(tokens_ref[...].astype(F32), gain_ref[...]).astype(BF16)
    slots = picks_ref.shape[1]
    here = lax.broadcasted_iota(jnp.int32, (rows, slots), 0) == picks_ref[...]
    onehot = jnp.where(here, 1.0, 0.0).astype(BF16)
    out_ref[...] = lax.dot_general(
        onehot, normed, (((0,), (0,)), ((), ())), preferred_element_type=F32
    ).astype(BF16)


def pick_rows(tokens, gain, picks):
    slots, width = picks.shape[1], tokens.shape[1]
    return pl.pallas_call(
        pick_kernel,
        in_specs=[_VM()] * 3,
        out_specs=_VM(),
        out_shape=jax.ShapeDtypeStruct((slots, width), BF16),
        compiler_params=pltpu.CompilerParams(vmem_limit_bytes=VMEM // 4),
    )(tokens, gain, picks)


def gelu(v):
    return 0.5 * v * (1.0 + jnp.tanh(0.7978845608028654 * (v + 0.044715 * (v * v * v))))


def expert_kernel(blocks, place, rows_ref, own_ref, *refs):
    ring = refs[:-7]
    early, late, out_ref, w_in, w_out, middle, sems = refs[-7:]
    block, turn = place[0], place[1]
    size = own_ref.shape[0] // 2

    def at(offset):
        return lax.rem(block + offset + blocks, blocks)

    def halves(ref, start, index):
        return [
            (ref.at[pl.ds(start + k * size, size)], buffer.at[index])
            for k, buffer in enumerate((w_in, w_out))
        ]

    jobs = [[], []]
    found = [halves(own_ref, 0, block)]
    for step, ref in enumerate(ring, 1):
        found.append(halves(ref, 0, at(-step * turn)))
    count = early.shape[0] // own_ref.shape[0]
    for step in range(1, len(ring)):
        ref, k = (early, step - 1) if step <= count else (late, step - 1 - count)
        found.append(halves(ref, k * own_ref.shape[0], at(step * turn)))
    for pair in found:
        for k in range(2):
            jobs[k].append(pair[k])
    copies = [
        [pltpu.make_async_copy(src, dst, sems.at[k, n]) for n, (src, dst) in enumerate(jobs[k])]
        for k in range(2)
    ]
    for part in copies:
        for copy in part:
            copy.start()
    width, hidden = rows_ref.shape[1], w_in.shape[2]
    tile = 256
    for copy in copies[0]:
        copy.wait()

    @pl.loop(0, rows_ref.shape[0] // tile)
    def _(i):
        here = pl.ds(pl.multiple_of(i * tile, tile), tile)
        middle[here, :] = gelu(
            jnp.dot(
                rows_ref[here, :], w_in[...].reshape(width, hidden), preferred_element_type=F32
            )
        ).astype(BF16)

    for copy in copies[1]:
        copy.wait()

    @pl.loop(0, rows_ref.shape[0] // tile)
    def _(i):
        here = pl.ds(pl.multiple_of(i * tile, tile), tile)
        out_ref[here, :] = lax.dot_general(
            middle[here, :],
            w_out[...].reshape(width, hidden),
            (((1,), (1,)), ((), ())),
            preferred_element_type=F32,
        ).astype(BF16)


def expert(blocks, place, rows, own, ring, early, late):
    total, width = rows.shape
    part, hidden = own.shape[0] // 2, own.shape[1]
    anywhere = pl.BlockSpec(memory_space=pl.ANY)
    return pl.pallas_call(
        functools.partial(expert_kernel, blocks),
        in_specs=[pl.BlockSpec(memory_space=pltpu.SMEM), _VM()]
        + [anywhere] * (3 + len(ring)),
        out_specs=_VM(),
        out_shape=jax.ShapeDtypeStruct((total, width), BF16),
        scratch_shapes=[
            pltpu.VMEM((blocks, part, hidden), BF16),
            pltpu.VMEM((blocks, part, hidden), BF16),
            pltpu.VMEM((total, hidden), BF16),
            pltpu.SemaphoreType.DMA((2, 2 * len(ring))),
        ],
        compiler_params=pltpu.CompilerParams(vmem_limit_bytes=VMEM // 2),
        cost_estimate=pl.CostEstimate(
            flops=4 * total * width * hidden,
            bytes_accessed=4 * width * hidden + 4 * total * width,
            transcendentals=total * hidden,
        ),
    )(place, rows, own, *ring, early, late)


def spread(mine, sizes):
    _, blocks, _, _, cores = sizes
    swap = [(0, 1), (1, 0)]
    core = lax.axis_index("core")
    other = lax.ppermute(mine, "core", swap)
    own = jnp.where(
        core == 0, jnp.concatenate([mine, other]), jnp.concatenate([other, mine])
    )
    turns = [
        (b * cores + c, (b + (1 if c == 0 else -1)) % blocks * cores + c)
        for b in range(blocks)
        for c in range(cores)
    ]
    steps = blocks // 2
    ring, held = [], own
    for _ in range(steps):
        held = lax.ppermute(held, ("block", "core"), turns)
        ring.append(held)
    cut = steps // 2
    early = lax.ppermute(jnp.concatenate(ring[:cut]), "core", swap)
    late = lax.ppermute(jnp.concatenate(ring[cut : steps - 1]), "core", swap)
    place = jnp.stack([lax.axis_index("block"), 1 - 2 * core]).astype(jnp.int32)
    return blocks, place, own, ring, early, late


def pieces(v, count):
    out = []
    for _ in range(count):
        part = v.astype(BF16)
        out.append(part)
        v = v - part.astype(F32)
    return out


def tail_kernel(
    back_ref, picks_ref, weight_ref, tokens_ref, gain_ref, key_ref, value_ref, query_ref,
    encoded_ref, packet_ref,
):
    rows = tokens_ref.shape[0]
    slots = picks_ref.shape[1]
    here = lax.broadcasted_iota(jnp.int32, (rows, slots), 0) == picks_ref[...]
    spread = jnp.where(here, weight_ref[...], 0.0)
    back = back_ref[...]
    expert_sum = sum(
        jnp.dot(part, back, preferred_element_type=F32) for part in pieces(spread, 3)
    )
    mixed = tokens_ref[...].astype(F32) + expert_sum
    encoded = rms_norm(mixed, gain_ref[...]).astype(BF16)
    encoded_ref[...] = encoded
    keys = jnp.dot(encoded, key_ref[...], preferred_element_type=F32).astype(BF16)
    values = jnp.dot(encoded, value_ref[...], preferred_element_type=F32).astype(BF16)
    query = query_ref[...]
    count, features = query.shape
    size = features // HEADS
    lane = lax.broadcasted_iota(jnp.int32, (rows, 2 * size), 1)
    low = lane < size
    zero = jnp.zeros((), BF16)
    stat_lane = lax.broadcasted_iota(jnp.int32, (count, 128), 1)
    stats = jnp.zeros((count, 128), F32)
    for pair in range(HEADS // 2):
        span = slice(pair * 2 * size, (pair + 1) * 2 * size)
        q, k, v = query[:, span], keys[:, span], values[:, span]
        total = None
        for odd in range(2):
            mask = low if odd == 0 else ~low
            scores = lax.dot_general(
                q,
                jnp.where(mask, k, zero),
                (((1,), (1,)), ((), ())),
                preferred_element_type=F32,
            ) * (size**-0.5)
            top = jnp.max(scores, axis=1, keepdims=True)
            weights = jnp.exp(scores - top)
            amount = jnp.sum(weights, axis=1, keepdims=True)
            term = jnp.dot(
                weights.astype(BF16), jnp.where(mask, v, zero), preferred_element_type=F32
            )
            total = term if total is None else total + term
            entries = pieces(top, 3) + pieces(amount, 2)
            for i, entry in enumerate(entries):
                at = (2 * pair + odd) * STATS + i
                stats = jnp.where(stat_lane == at, entry.astype(F32), stats)
        packet_ref[:, span] = total.astype(BF16)
    packet_ref[:, features:] = stats.astype(BF16)


def tail(back, picks, weight, tokens, gain, w_key, w_value, query):
    rows, width = tokens.shape
    count, features = query.shape
    return pl.pallas_call(
        tail_kernel,
        in_specs=[_VM()] * 8,
        out_specs=(_VM(), _VM()),
        out_shape=(
            jax.ShapeDtypeStruct((rows, width), BF16),
            jax.ShapeDtypeStruct((count, features + 128), BF16),
        ),
        compiler_params=pltpu.CompilerParams(vmem_limit_bytes=VMEM // 2),
    )(back, picks, weight, tokens, gain, w_key, w_value, query)


def merge_kernel(got_ref, proj_ref, out_ref):
    group, count, wide = got_ref.shape
    features = wide - 128
    size = features // HEADS
    lane = lax.broadcasted_iota(jnp.int32, (count, 2 * size), 1)
    low = lane < size
    stats = [got_ref[g, :, features:].astype(F32) for g in range(group)]
    parts = []
    for pair in range(HEADS // 2):
        span = slice(pair * 2 * size, (pair + 1) * 2 * size)
        scales, totals = [], []
        for odd in range(2):
            at = (2 * pair + odd) * STATS
            tops = [s[:, at : at + 1] + s[:, at + 1 : at + 2] + s[:, at + 2 : at + 3] for s in stats]
            amounts = [s[:, at + 3 : at + 4] + s[:, at + 4 : at + 5] for s in stats]
            top = functools.reduce(jnp.maximum, tops)
            scale = [jnp.exp(t - top) for t in tops]
            scales.append(scale)
            totals.append(sum(a * s for a, s in zip(amounts, scale)))
        weighted = sum(
            got_ref[g, :, span].astype(F32) * jnp.where(low, scales[0][g], scales[1][g])
            for g in range(group)
        )
        parts.append((weighted / jnp.where(low, totals[0], totals[1])).astype(BF16))
    context = jnp.concatenate(parts, axis=1)
    out_ref[...] = jnp.dot(context, proj_ref[...], preferred_element_type=F32).astype(BF16)


def merge(got, w_proj):
    return pl.pallas_call(
        merge_kernel,
        in_specs=[_VM()] * 2,
        out_specs=_VM(),
        out_shape=jax.ShapeDtypeStruct((got.shape[1], w_proj.shape[1]), BF16),
        compiler_params=pltpu.CompilerParams(vmem_limit_bytes=VMEM // 4),
    )(got, w_proj)


def scatter_pairs(sizes):
    dps, blocks, parities, rows, cores = sizes
    plane = dps * rows * cores

    def place(dp, z, row, core):
        return ((dp * blocks * parities + z) * rows + row) * cores + core

    pairs = []
    for dp in range(dps):
        for parity in range(parities):
            for row in range(rows):
                e = (dp * parities + parity) * rows + row
                for block in range(blocks):
                    for core in range(cores):
                        j = block * cores + core
                        column = (STEP_J * j + STEP_E * e) % plane
                        source = place(
                            column // (rows * cores), e, column // cores % rows, column % cores
                        )
                        pairs.append((source, place(dp, block * parities + parity, row, core)))
    return pairs


def local(
    sizes, tokens, picks, gates, counts, norm_in, norm_out, w_in, w_out, w_key, w_value, queries, w_proj
):
    dps, blocks, parities, row_count, cores = sizes
    plane = dps * row_count * cores
    experts, cap = picks.shape[1], picks.shape[2]
    width = tokens.shape[1]
    own = lax.axis_index("block") * parities + lax.axis_index("parity")
    column = (lax.axis_index("dp") * row_count + lax.axis_index("row")) * cores + lax.axis_index(
        "core"
    )
    j = (INV_J * (column + (plane - STEP_E) * own)) % plane
    shard = take_shard(jnp.stack([j // cores, j % cores]).astype(jnp.int32), w_in, w_out, blocks)
    shard = lax.ppermute(shard, ALL, scatter_pairs(sizes))
    query = lax.all_gather(queries, SEQ, tiled=True)
    shard, query, picks = lax.optimization_barrier((shard, query, picks))
    blocks, place, own_part, ring, early, late = spread(shard, sizes)

    pick_row = picks.reshape(1, experts * cap)
    live = lax.broadcasted_iota(jnp.int32, (experts, cap), 1) < counts[0][:, None]
    slot_weight = jnp.where(live, gates[0], 0.0).reshape(1, experts * cap)
    chosen = pick_rows(tokens, norm_in[None, :], pick_row)
    near = experts * cores
    there = lax.all_to_all(
        chosen.reshape(near, -1, width), NEAR, split_axis=0, concat_axis=0, tiled=True
    )
    result = expert(blocks, place, there.reshape(-1, width), own_part, ring, early, late)
    back = lax.all_to_all(
        result.reshape(near, -1, width), NEAR, split_axis=0, concat_axis=0, tiled=True
    ).reshape(-1, width)
    encoded, packet = tail(
        back, pick_row, slot_weight, tokens, norm_out[None, :], w_key, w_value, query
    )
    group = row_count * cores
    got = lax.all_to_all(
        packet.reshape(group, -1, packet.shape[1]), SEQ, split_axis=0, concat_axis=0, tiled=True
    )
    return encoded, merge(got, w_proj)


def solution(mesh):
    dps, planes, seq = mesh.shape["dp"], mesh.shape["expert"], mesh.shape["seq"]
    sizes = (dps, planes // BLOCK, BLOCK, seq // 2, 2)
    split = Mesh(mesh.devices.reshape(sizes), ALL)
    in_specs = (
        P(ALL, None),
        P(ALL, None, None),
        P(ALL, None, None),
        P(ALL, None),
        P(),
        P(),
        P(("block", "parity"), None, None),
        P(("block", "parity"), None, None),
        P(),
        P(),
        P(ALL, None),
        P(),
    )
    out_specs = (P(ALL, None), P(ALL, None))
    return jax.shard_map(
        functools.partial(local, sizes),
        mesh=split,
        in_specs=in_specs,
        out_specs=out_specs,
        check_vma=False,
    )
```

```python
import functools

import jax
import jax.numpy as jnp
from jax import lax
from jax.experimental import pallas as pl
from jax.experimental.pallas import tpu as pltpu
from jax.sharding import Mesh
from jax.sharding import PartitionSpec as P

HEADS = 8
EPSILON = 1e-06
BLOCK = 2
ALL = ("dp", "block", "parity", "row", "core")
NEAR = ("dp", "parity", "row")
SEQ = ("row", "core")
STEP_J, STEP_E, INV_J = 9, 30, 25
STATS = 5
VMEM = 60 * 1024 * 1024
FULL = 61 * 1024 * 1024
F32 = jnp.float32
BF16 = jnp.bfloat16

_VM = functools.partial(pl.BlockSpec, memory_space=pltpu.VMEM)


def rms_norm(values, gain):
    mean_square = jnp.mean(values * values, axis=-1, keepdims=True)
    return values * lax.rsqrt(mean_square + EPSILON) * gain


def shard_kernel(which, w_in_ref, w_out_ref, out_ref):
    rows = out_ref.shape[0]
    block, kind = which[0], which[1]

    @pl.when(kind == 0)
    def _():
        out_ref[...] = w_in_ref[0]

    @pl.when(kind == 1)
    def _():
        turned = w_out_ref[0].astype(F32).T
        upper = jnp.where(block % 2 == 1, turned[rows:], turned[:rows])
        out_ref[...] = upper.astype(BF16)


def take_shard(which, w_in, w_out, blocks):
    width, hidden = w_in.shape[1], w_in.shape[2]
    rows = width // blocks
    return pl.pallas_call(
        shard_kernel,
        grid_spec=pltpu.PrefetchScalarGridSpec(
            num_scalar_prefetch=1,
            grid=(1,),
            in_specs=[
                pl.BlockSpec((1, rows, hidden), lambda i, s: (0, s[0], 0)),
                pl.BlockSpec((1, hidden, 2 * rows), lambda i, s: (0, 0, s[0] // 2)),
            ],
            out_specs=pl.BlockSpec((rows, hidden), lambda i, s: (0, 0)),
        ),
        out_shape=jax.ShapeDtypeStruct((rows, hidden), BF16),
        compiler_params=pltpu.CompilerParams(vmem_limit_bytes=FULL),
    )(which, w_in, w_out)


def pick_kernel(tokens_ref, gain_ref, picks_ref, out_ref):
    rows = tokens_ref.shape[0]
    normed = rms_norm(tokens_ref[...].astype(F32), gain_ref[...]).astype(BF16)
    slots = picks_ref.shape[1]
    here = lax.broadcasted_iota(jnp.int32, (rows, slots), 0) == picks_ref[...]
    onehot = jnp.where(here, 1.0, 0.0).astype(BF16)
    out_ref[...] = lax.dot_general(
        onehot, normed, (((0,), (0,)), ((), ())), preferred_element_type=F32
    ).astype(BF16)


def pick_rows(tokens, gain, picks):
    slots, width = picks.shape[1], tokens.shape[1]
    return pl.pallas_call(
        pick_kernel,
        in_specs=[_VM()] * 3,
        out_specs=_VM(),
        out_shape=jax.ShapeDtypeStruct((slots, width), BF16),
        compiler_params=pltpu.CompilerParams(vmem_limit_bytes=VMEM // 4),
    )(tokens, gain, picks)


def gelu(v):
    return 0.5 * v * (1.0 + jnp.tanh(0.7978845608028654 * (v + 0.044715 * (v * v * v))))


def expert_kernel(blocks, place, rows_ref, own_ref, *refs):
    parts = refs[:-5]
    out_ref, w_in, w_out, middle, sems = refs[-5:]
    ring, twins = parts[: blocks // 2], parts[blocks // 2 :]
    block, turn = place[0], place[1]
    size = own_ref.shape[0] // 2

    def at(offset):
        return lax.rem(block + offset + blocks, blocks)

    def halves(ref, index):
        return [
            (ref.at[pl.ds(k * size, size)], buffer.at[index])
            for k, buffer in enumerate((w_in, w_out))
        ]

    jobs = [[], []]
    found = [halves(own_ref, block)]
    for step, ref in enumerate(ring, 1):
        found.append(halves(ref, at(-step * turn)))
    for step, ref in enumerate(twins, 1):
        found.append(halves(ref, at(step * turn)))
    for pair in found:
        for k in range(2):
            jobs[k].append(pair[k])
    copies = [
        [pltpu.make_async_copy(src, dst, sems.at[k, n]) for n, (src, dst) in enumerate(jobs[k])]
        for k in range(2)
    ]
    for part in copies:
        for copy in part:
            copy.start()
    width, hidden = rows_ref.shape[1], w_in.shape[2]
    step = 512
    for copy in copies[0]:
        copy.wait()
    rows = rows_ref[...]
    for start in range(0, hidden, step):
        span = slice(start, min(start + step, hidden))
        first = w_in[:, :, span].reshape(width, -1)
        middle[:, span] = gelu(jnp.dot(rows, first, preferred_element_type=F32)).astype(BF16)
    for copy in copies[1]:
        copy.wait()
    mid = middle[...]
    for start in range(0, width, step):
        second = w_out[start // size : (start + step) // size].reshape(step, hidden)
        out_ref[:, start : start + step] = lax.dot_general(
            mid, second, (((1,), (1,)), ((), ())), preferred_element_type=F32
        ).astype(BF16)


def expert(blocks, place, rows, own, ring, twins):
    total, width = rows.shape
    part, hidden = own.shape[0] // 2, own.shape[1]
    anywhere = pl.BlockSpec(memory_space=pl.ANY)
    return pl.pallas_call(
        functools.partial(expert_kernel, blocks),
        in_specs=[pl.BlockSpec(memory_space=pltpu.SMEM), _VM()]
        + [anywhere] * (1 + len(ring) + len(twins)),
        out_specs=_VM(),
        out_shape=jax.ShapeDtypeStruct((total, width), BF16),
        scratch_shapes=[
            pltpu.VMEM((blocks, part, hidden), BF16),
            pltpu.VMEM((blocks, part, hidden), BF16),
            pltpu.VMEM((total, hidden), BF16),
            pltpu.SemaphoreType.DMA((2, 2 * len(ring))),
        ],
        compiler_params=pltpu.CompilerParams(vmem_limit_bytes=FULL),
        cost_estimate=pl.CostEstimate(
            flops=4 * total * width * hidden,
            bytes_accessed=4 * width * hidden + 4 * total * width,
            transcendentals=total * hidden,
        ),
    )(place, rows, own, *ring, *twins)


def spread(mine, sizes):
    _, blocks, _, _, cores = sizes
    swap = [(0, 1), (1, 0)]
    core = lax.axis_index("core")
    other = lax.ppermute(mine, "core", swap)
    own = jnp.where(
        core == 0, jnp.concatenate([mine, other]), jnp.concatenate([other, mine])
    )
    turns = [
        (b * cores + c, (b + (1 if c == 0 else -1)) % blocks * cores + c)
        for b in range(blocks)
        for c in range(cores)
    ]
    steps = blocks // 2
    ring, held = [], own
    for _ in range(steps):
        held = lax.ppermute(held, ("block", "core"), turns)
        ring.append(held)
    twins = [lax.ppermute(held, "core", swap) for held in ring[:-1]]
    place = jnp.stack([lax.axis_index("block"), 1 - 2 * core]).astype(jnp.int32)
    return blocks, place, own, ring, twins


def pieces(v, count):
    out = []
    for _ in range(count):
        part = v.astype(BF16)
        out.append(part)
        v = v - part.astype(F32)
    return out


def tail_kernel(
    back_ref, picks_ref, weight_ref, tokens_ref, gain_ref, key_ref, value_ref, query_ref,
    encoded_ref, packet_ref,
):
    rows = tokens_ref.shape[0]
    slots = picks_ref.shape[1]
    here = lax.broadcasted_iota(jnp.int32, (rows, slots), 0) == picks_ref[...]
    spread = jnp.where(here, weight_ref[...], 0.0)
    back = back_ref[...]
    expert_sum = sum(
        jnp.dot(part, back, preferred_element_type=F32) for part in pieces(spread, 3)
    )
    mixed = tokens_ref[...].astype(F32) + expert_sum
    encoded = rms_norm(mixed, gain_ref[...]).astype(BF16)
    encoded_ref[...] = encoded
    keys = jnp.dot(encoded, key_ref[...], preferred_element_type=F32).astype(BF16)
    values = jnp.dot(encoded, value_ref[...], preferred_element_type=F32).astype(BF16)
    query = query_ref[...]
    count, features = query.shape
    size = features // HEADS
    lane = lax.broadcasted_iota(jnp.int32, (rows, 2 * size), 1)
    low = lane < size
    zero = jnp.zeros((), BF16)
    stat_lane = lax.broadcasted_iota(jnp.int32, (count, 128), 1)
    stats = jnp.zeros((count, 128), F32)
    for pair in range(HEADS // 2):
        span = slice(pair * 2 * size, (pair + 1) * 2 * size)
        q, k, v = query[:, span], keys[:, span], values[:, span]
        total = None
        for odd in range(2):
            mask = low if odd == 0 else ~low
            scores = lax.dot_general(
                q,
                jnp.where(mask, k, zero),
                (((1,), (1,)), ((), ())),
                preferred_element_type=F32,
            ) * (size**-0.5)
            top = jnp.max(scores, axis=1, keepdims=True)
            weights = jnp.exp(scores - top)
            amount = jnp.sum(weights, axis=1, keepdims=True)
            term = jnp.dot(
                weights.astype(BF16), jnp.where(mask, v, zero), preferred_element_type=F32
            )
            total = term if total is None else total + term
            entries = pieces(top, 3) + pieces(amount, 2)
            for i, entry in enumerate(entries):
                at = (2 * pair + odd) * STATS + i
                stats = jnp.where(stat_lane == at, entry.astype(F32), stats)
        packet_ref[:, span] = total.astype(BF16)
    packet_ref[:, features:] = stats.astype(BF16)


def tail(back, picks, weight, tokens, gain, w_key, w_value, query):
    rows, width = tokens.shape
    count, features = query.shape
    return pl.pallas_call(
        tail_kernel,
        in_specs=[_VM()] * 8,
        out_specs=(_VM(), _VM()),
        out_shape=(
            jax.ShapeDtypeStruct((rows, width), BF16),
            jax.ShapeDtypeStruct((count, features + 128), BF16),
        ),
        compiler_params=pltpu.CompilerParams(vmem_limit_bytes=VMEM // 2),
    )(back, picks, weight, tokens, gain, w_key, w_value, query)


def merge_kernel(got_ref, proj_ref, out_ref):
    group, count, wide = got_ref.shape
    features = wide - 128
    size = features // HEADS
    lane = lax.broadcasted_iota(jnp.int32, (count, 2 * size), 1)
    low = lane < size
    stats = [got_ref[g, :, features:].astype(F32) for g in range(group)]
    parts = []
    for pair in range(HEADS // 2):
        span = slice(pair * 2 * size, (pair + 1) * 2 * size)
        scales, totals = [], []
        for odd in range(2):
            at = (2 * pair + odd) * STATS
            tops = [s[:, at : at + 1] + s[:, at + 1 : at + 2] + s[:, at + 2 : at + 3] for s in stats]
            amounts = [s[:, at + 3 : at + 4] + s[:, at + 4 : at + 5] for s in stats]
            top = functools.reduce(jnp.maximum, tops)
            scale = [jnp.exp(t - top) for t in tops]
            scales.append(scale)
            totals.append(sum(a * s for a, s in zip(amounts, scale)))
        weighted = sum(
            got_ref[g, :, span].astype(F32) * jnp.where(low, scales[0][g], scales[1][g])
            for g in range(group)
        )
        parts.append((weighted / jnp.where(low, totals[0], totals[1])).astype(BF16))
    context = jnp.concatenate(parts, axis=1)
    out_ref[...] = jnp.dot(context, proj_ref[...], preferred_element_type=F32).astype(BF16)


def merge(got, w_proj):
    return pl.pallas_call(
        merge_kernel,
        in_specs=[_VM()] * 2,
        out_specs=_VM(),
        out_shape=jax.ShapeDtypeStruct((got.shape[1], w_proj.shape[1]), BF16),
        compiler_params=pltpu.CompilerParams(vmem_limit_bytes=VMEM // 4),
    )(got, w_proj)


def scatter_pairs(sizes):
    dps, blocks, parities, rows, cores = sizes
    plane = dps * rows * cores

    def place(dp, z, row, core):
        return ((dp * blocks * parities + z) * rows + row) * cores + core

    pairs = []
    for dp in range(dps):
        for parity in range(parities):
            for row in range(rows):
                e = (dp * parities + parity) * rows + row
                for block in range(blocks):
                    for core in range(cores):
                        j = block * cores + core
                        column = (STEP_J * j + STEP_E * e) % plane
                        source = place(
                            column // (rows * cores), e, column // cores % rows, column % cores
                        )
                        pairs.append((source, place(dp, block * parities + parity, row, core)))
    return pairs


def local(
    sizes, tokens, picks, gates, counts, norm_in, norm_out, w_in, w_out, w_key, w_value, queries, w_proj
):
    dps, blocks, parities, row_count, cores = sizes
    plane = dps * row_count * cores
    experts, cap = picks.shape[1], picks.shape[2]
    width = tokens.shape[1]
    own = lax.axis_index("block") * parities + lax.axis_index("parity")
    column = (lax.axis_index("dp") * row_count + lax.axis_index("row")) * cores + lax.axis_index(
        "core"
    )
    j = (INV_J * (column + (plane - STEP_E) * own)) % plane
    shard = take_shard(jnp.stack([j // cores, j % cores]).astype(jnp.int32), w_in, w_out, blocks)
    shard = lax.ppermute(shard, ALL, scatter_pairs(sizes))
    query = lax.all_gather(queries, SEQ, tiled=True)
    shard, query, picks = lax.optimization_barrier((shard, query, picks))
    blocks, place, own_part, ring, twins = spread(shard, sizes)

    pick_row = picks.reshape(1, experts * cap)
    live = lax.broadcasted_iota(jnp.int32, (experts, cap), 1) < counts[0][:, None]
    slot_weight = jnp.where(live, gates[0], 0.0).reshape(1, experts * cap)
    chosen = pick_rows(tokens, norm_in[None, :], pick_row)
    there = lax.all_to_all(
        chosen.reshape(experts, -1, width), NEAR, split_axis=0, concat_axis=0, tiled=True
    )
    result = expert(blocks, place, there.reshape(-1, width), own_part, ring, twins)
    back = lax.all_to_all(
        result.reshape(experts, -1, width), NEAR, split_axis=0, concat_axis=0, tiled=True
    ).reshape(-1, width)
    encoded, packet = tail(
        back, pick_row, slot_weight, tokens, norm_out[None, :], w_key, w_value, query
    )
    group = row_count * cores
    got = lax.all_to_all(
        packet.reshape(group, -1, packet.shape[1]), SEQ, split_axis=0, concat_axis=0, tiled=True
    )
    return encoded, merge(got, w_proj)


def solution(mesh):
    dps, planes, seq = mesh.shape["dp"], mesh.shape["expert"], mesh.shape["seq"]
    sizes = (dps, planes // BLOCK, BLOCK, seq // 2, 2)
    split = Mesh(mesh.devices.reshape(sizes), ALL)
    in_specs = (
        P(ALL, None),
        P(ALL, None, None),
        P(ALL, None, None),
        P(ALL, None),
        P(),
        P(),
        P(("block", "parity"), None, None),
        P(("block", "parity"), None, None),
        P(),
        P(),
        P(ALL, None),
        P(),
    )
    out_specs = (P(ALL, None), P(ALL, None))
    return jax.shard_map(
        functools.partial(local, sizes),
        mesh=split,
        in_specs=in_specs,
        out_specs=out_specs,
        check_vma=False,
    )
```

```python
import functools

import jax
import jax.numpy as jnp
from jax import lax
from jax.experimental import pallas as pl
from jax.experimental.pallas import tpu as pltpu
from jax.sharding import Mesh
from jax.sharding import PartitionSpec as P

HEADS = 8
EPSILON = 1e-06
BLOCK = 2
ALL = ("dp", "block", "parity", "row", "core")
NEAR = ("dp", "parity", "row")
SEQ = ("row", "core")
STEP_J, STEP_E, INV_J = 9, 30, 25
STATS = 5
STEP = 512
VMEM = 60 * 1024 * 1024
FULL = 61 * 1024 * 1024
F32 = jnp.float32
BF16 = jnp.bfloat16

_VM = functools.partial(pl.BlockSpec, memory_space=pltpu.VMEM)


def rms_norm(values, gain):
    mean_square = jnp.mean(values * values, axis=-1, keepdims=True)
    return values * lax.rsqrt(mean_square + EPSILON) * gain


def shard_kernel(which, w_in_ref, w_out_ref, out_ref):
    rows = out_ref.shape[0]
    block, kind = which[0], which[1]

    @pl.when(kind == 0)
    def _():
        out_ref[...] = w_in_ref[0]

    @pl.when(kind == 1)
    def _():
        turned = w_out_ref[0].astype(F32).T
        upper = jnp.where(block % 2 == 1, turned[rows:], turned[:rows])
        out_ref[...] = upper.astype(BF16)


def take_shard(which, w_in, w_out, blocks):
    width, hidden = w_in.shape[1], w_in.shape[2]
    rows = width // blocks
    return pl.pallas_call(
        shard_kernel,
        grid_spec=pltpu.PrefetchScalarGridSpec(
            num_scalar_prefetch=1,
            grid=(1,),
            in_specs=[
                pl.BlockSpec((1, rows, hidden), lambda i, s: (0, s[0], 0)),
                pl.BlockSpec((1, hidden, 2 * rows), lambda i, s: (0, 0, s[0] // 2)),
            ],
            out_specs=pl.BlockSpec((rows, hidden), lambda i, s: (0, 0)),
        ),
        out_shape=jax.ShapeDtypeStruct((rows, hidden), BF16),
        compiler_params=pltpu.CompilerParams(vmem_limit_bytes=FULL),
    )(which, w_in, w_out)


def pick_kernel(tokens_ref, gain_ref, picks_ref, out_ref):
    rows = tokens_ref.shape[0]
    normed = rms_norm(tokens_ref[...].astype(F32), gain_ref[...]).astype(BF16)
    slots = picks_ref.shape[1]
    here = lax.broadcasted_iota(jnp.int32, (rows, slots), 0) == picks_ref[...]
    onehot = jnp.where(here, 1.0, 0.0).astype(BF16)
    out_ref[...] = lax.dot_general(
        onehot, normed, (((0,), (0,)), ((), ())), preferred_element_type=F32
    ).astype(BF16)


def pick_rows(tokens, gain, picks):
    slots, width = picks.shape[1], tokens.shape[1]
    return pl.pallas_call(
        pick_kernel,
        in_specs=[_VM()] * 3,
        out_specs=_VM(),
        out_shape=jax.ShapeDtypeStruct((slots, width), BF16),
        compiler_params=pltpu.CompilerParams(vmem_limit_bytes=VMEM // 4),
    )(tokens, gain, picks)


def gelu(v):
    return 0.5 * v * (1.0 + jnp.tanh(0.7978845608028654 * (v + 0.044715 * (v * v * v))))


def expert_kernel(rows_ref, weights_ref, out_ref, w_in, w_out, middle, sems):
    blocks, _, part, hidden = weights_ref.shape
    width = blocks * part
    inner = [pl.ds(i, min(STEP, hidden - i)) for i in range(0, hidden, STEP)]
    outer = [pl.ds(i, STEP // part) for i in range(0, blocks, STEP // part)]
    copies = [
        pltpu.make_async_copy(weights_ref.at[:, 0, :, span], w_in.at[:, :, span], sems.at[n])
        for n, span in enumerate(inner)
    ] + [
        pltpu.make_async_copy(
            weights_ref.at[span, 1], w_out.at[span], sems.at[len(inner) + n]
        )
        for n, span in enumerate(outer)
    ]
    for copy in copies:
        copy.start()
    rows = rows_ref[...]
    for n, span in enumerate(inner):
        copies[n].wait()
        first = w_in[:, :, span].reshape(width, -1)
        middle[:, span] = gelu(jnp.dot(rows, first, preferred_element_type=F32)).astype(BF16)
    mid = middle[...]
    for n, span in enumerate(outer):
        copies[len(inner) + n].wait()
        out_ref[:, n * STEP : (n + 1) * STEP] = lax.dot_general(
            mid,
            w_out[span].reshape(STEP, hidden),
            (((1,), (1,)), ((), ())),
            preferred_element_type=F32,
        ).astype(BF16)


def expert(rows, weights):
    total, width = rows.shape
    blocks, _, part, hidden = weights.shape
    return pl.pallas_call(
        expert_kernel,
        in_specs=[_VM(), pl.BlockSpec(memory_space=pltpu.HBM)],
        out_specs=_VM(),
        out_shape=jax.ShapeDtypeStruct((total, width), BF16),
        scratch_shapes=[
            pltpu.VMEM((blocks, part, hidden), BF16),
            pltpu.VMEM((blocks, part, hidden), BF16),
            pltpu.VMEM((total, hidden), BF16),
            pltpu.SemaphoreType.DMA((-(-hidden // STEP) + width // STEP,)),
        ],
        compiler_params=pltpu.CompilerParams(vmem_limit_bytes=VMEM // 2),
        cost_estimate=pl.CostEstimate(
            flops=4 * total * width * hidden,
            bytes_accessed=4 * width * hidden + 4 * total * width,
            transcendentals=total * hidden,
        ),
    )(rows, weights)


def pieces(v, count):
    out = []
    for _ in range(count):
        part = v.astype(BF16)
        out.append(part)
        v = v - part.astype(F32)
    return out


def tail_kernel(
    back_ref, picks_ref, weight_ref, tokens_ref, gain_ref, key_ref, value_ref, query_ref,
    encoded_ref, packet_ref, value_held, value_sem,
):
    value_copy = pltpu.make_async_copy(value_ref, value_held, value_sem)
    value_copy.start()
    rows = tokens_ref.shape[0]
    slots = picks_ref.shape[1]
    here = lax.broadcasted_iota(jnp.int32, (rows, slots), 0) == picks_ref[...]
    spread = jnp.where(here, weight_ref[...], 0.0)
    back = back_ref[...]
    expert_sum = sum(
        jnp.dot(part, back, preferred_element_type=F32) for part in pieces(spread, 3)
    )
    mixed = tokens_ref[...].astype(F32) + expert_sum
    encoded = rms_norm(mixed, gain_ref[...]).astype(BF16)
    encoded_ref[...] = encoded
    keys = jnp.dot(encoded, key_ref[...], preferred_element_type=F32).astype(BF16)
    value_copy.wait()
    values = jnp.dot(encoded, value_held[...], preferred_element_type=F32).astype(BF16)
    query = query_ref[...]
    count, features = query.shape
    size = features // HEADS
    lane = lax.broadcasted_iota(jnp.int32, (rows, 2 * size), 1)
    low = lane < size
    zero = jnp.zeros((), BF16)
    stat_lane = lax.broadcasted_iota(jnp.int32, (count, 128), 1)
    stats = jnp.zeros((count, 128), F32)
    for pair in range(HEADS // 2):
        span = slice(pair * 2 * size, (pair + 1) * 2 * size)
        q, k, v = query[:, span], keys[:, span], values[:, span]
        total = None
        for odd in range(2):
            mask = low if odd == 0 else ~low
            scores = lax.dot_general(
                q,
                jnp.where(mask, k, zero),
                (((1,), (1,)), ((), ())),
                preferred_element_type=F32,
            ) * (size**-0.5)
            top = jnp.max(scores, axis=1, keepdims=True)
            weights = jnp.exp(scores - top)
            amount = jnp.sum(weights, axis=1, keepdims=True)
            term = jnp.dot(
                weights.astype(BF16), jnp.where(mask, v, zero), preferred_element_type=F32
            )
            total = term if total is None else total + term
            entries = pieces(top, 3) + pieces(amount, 2)
            for i, entry in enumerate(entries):
                at = (2 * pair + odd) * STATS + i
                stats = jnp.where(stat_lane == at, entry.astype(F32), stats)
        packet_ref[:, span] = total.astype(BF16)
    packet_ref[:, features:] = stats.astype(BF16)


def tail(back, picks, weight, tokens, gain, w_key, w_value, query):
    rows, width = tokens.shape
    count, features = query.shape
    return pl.pallas_call(
        tail_kernel,
        in_specs=[_VM()] * 6 + [pl.BlockSpec(memory_space=pltpu.HBM), _VM()],
        out_specs=(_VM(), _VM()),
        scratch_shapes=[pltpu.VMEM(w_value.shape, BF16), pltpu.SemaphoreType.DMA(())],
        out_shape=(
            jax.ShapeDtypeStruct((rows, width), BF16),
            jax.ShapeDtypeStruct((count, features + 128), BF16),
        ),
        compiler_params=pltpu.CompilerParams(vmem_limit_bytes=VMEM // 2),
    )(back, picks, weight, tokens, gain, w_key, w_value, query)


def merge_kernel(got_ref, proj_ref, out_ref):
    group, count, wide = got_ref.shape
    features = wide - 128
    size = features // HEADS
    lane = lax.broadcasted_iota(jnp.int32, (count, 2 * size), 1)
    low = lane < size
    stats = [got_ref[g, :, features:].astype(F32) for g in range(group)]
    parts = []
    for pair in range(HEADS // 2):
        span = slice(pair * 2 * size, (pair + 1) * 2 * size)
        scales, totals = [], []
        for odd in range(2):
            at = (2 * pair + odd) * STATS
            tops = [s[:, at : at + 1] + s[:, at + 1 : at + 2] + s[:, at + 2 : at + 3] for s in stats]
            amounts = [s[:, at + 3 : at + 4] + s[:, at + 4 : at + 5] for s in stats]
            top = functools.reduce(jnp.maximum, tops)
            scale = [jnp.exp(t - top) for t in tops]
            scales.append(scale)
            totals.append(sum(a * s for a, s in zip(amounts, scale)))
        weighted = sum(
            got_ref[g, :, span].astype(F32) * jnp.where(low, scales[0][g], scales[1][g])
            for g in range(group)
        )
        parts.append((weighted / jnp.where(low, totals[0], totals[1])).astype(BF16))
    context = jnp.concatenate(parts, axis=1)
    out_ref[...] = jnp.dot(context, proj_ref[...], preferred_element_type=F32).astype(BF16)


def merge(got, w_proj):
    return pl.pallas_call(
        merge_kernel,
        in_specs=[_VM()] * 2,
        out_specs=_VM(),
        out_shape=jax.ShapeDtypeStruct((got.shape[1], w_proj.shape[1]), BF16),
        compiler_params=pltpu.CompilerParams(vmem_limit_bytes=VMEM // 4),
    )(got, w_proj)


def scatter_pairs(sizes):
    dps, blocks, parities, rows, cores = sizes
    plane = dps * rows * cores

    def place(dp, z, row, core):
        return ((dp * blocks * parities + z) * rows + row) * cores + core

    pairs = []
    for dp in range(dps):
        for parity in range(parities):
            for row in range(rows):
                e = (dp * parities + parity) * rows + row
                for block in range(blocks):
                    for core in range(cores):
                        j = block * cores + core
                        column = (STEP_J * j + STEP_E * e) % plane
                        source = place(
                            column // (rows * cores), e, column // cores % rows, column % cores
                        )
                        pairs.append((source, place(dp, block * parities + parity, row, core)))
    return pairs


def local(
    sizes, tokens, picks, gates, counts, norm_in, norm_out, w_in, w_out, w_key, w_value, queries, w_proj
):
    dps, blocks, parities, row_count, cores = sizes
    plane = dps * row_count * cores
    experts, cap = picks.shape[1], picks.shape[2]
    width = tokens.shape[1]
    own = lax.axis_index("block") * parities + lax.axis_index("parity")
    column = (lax.axis_index("dp") * row_count + lax.axis_index("row")) * cores + lax.axis_index(
        "core"
    )
    j = (INV_J * (column + (plane - STEP_E) * own)) % plane
    shard = take_shard(jnp.stack([j // cores, j % cores]).astype(jnp.int32), w_in, w_out, blocks)
    shard = lax.ppermute(shard, ALL, scatter_pairs(sizes))
    query = lax.all_gather(queries, SEQ, tiled=True)
    shard, query = lax.optimization_barrier((shard, query))
    weights = lax.all_gather(shard, ("block", "core"))
    weights = weights.reshape(blocks, cores, *shard.shape)

    pick_row = picks.reshape(1, experts * cap)
    live = lax.broadcasted_iota(jnp.int32, (experts, cap), 1) < counts[0][:, None]
    slot_weight = jnp.where(live, gates[0], 0.0).reshape(1, experts * cap)
    chosen = pick_rows(tokens, norm_in[None, :], pick_row)
    there = lax.all_to_all(
        chosen.reshape(experts, -1, width), NEAR, split_axis=0, concat_axis=0, tiled=True
    )
    result = expert(there.reshape(-1, width), weights)
    back = lax.all_to_all(
        result.reshape(experts, -1, width), NEAR, split_axis=0, concat_axis=0, tiled=True
    ).reshape(-1, width)
    encoded, packet = tail(
        back, pick_row, slot_weight, tokens, norm_out[None, :], w_key, w_value, query
    )
    group = row_count * cores
    got = lax.all_to_all(
        packet.reshape(group, -1, packet.shape[1]), SEQ, split_axis=0, concat_axis=0, tiled=True
    )
    return encoded, merge(got, w_proj)


def solution(mesh):
    dps, planes, seq = mesh.shape["dp"], mesh.shape["expert"], mesh.shape["seq"]
    sizes = (dps, planes // BLOCK, BLOCK, seq // 2, 2)
    split = Mesh(mesh.devices.reshape(sizes), ALL)
    in_specs = (
        P(ALL, None),
        P(ALL, None, None),
        P(ALL, None, None),
        P(ALL, None),
        P(),
        P(),
        P(("block", "parity"), None, None),
        P(("block", "parity"), None, None),
        P(),
        P(),
        P(ALL, None),
        P(),
    )
    out_specs = (P(ALL, None), P(ALL, None))
    return jax.shard_map(
        functools.partial(local, sizes),
        mesh=split,
        in_specs=in_specs,
        out_specs=out_specs,
        check_vma=False,
    )
```

```python
import functools

import jax
import jax.numpy as jnp
from jax import lax
from jax.experimental import pallas as pl
from jax.experimental.pallas import tpu as pltpu
from jax.sharding import Mesh
from jax.sharding import PartitionSpec as P

HEADS = 8
EPSILON = 1e-06
BLOCK = 2
ALL = ("dp", "block", "parity", "row", "core")
NEAR = ("dp", "parity", "row")
SEQ = ("row", "core")
STEP_J, STEP_E, INV_J = 9, 30, 25
STATS = 5
STEP = 512
VMEM = 60 * 1024 * 1024
FULL = 61 * 1024 * 1024
F32 = jnp.float32
BF16 = jnp.bfloat16

_VM = functools.partial(pl.BlockSpec, memory_space=pltpu.VMEM)


def rms_norm(values, gain):
    mean_square = jnp.mean(values * values, axis=-1, keepdims=True)
    return values * lax.rsqrt(mean_square + EPSILON) * gain


def shard_kernel(which, w_in_ref, w_out_ref, out_ref, columns, sem):
    rows = out_ref.shape[0]
    block, kind = which[0], which[1]

    @pl.when(kind == 0)
    def _():
        here = pl.ds(pl.multiple_of(block * rows, rows), rows)
        copy = pltpu.make_async_copy(w_in_ref.at[0, here, :], out_ref, sem)
        copy.start()
        copy.wait()

    @pl.when(kind == 1)
    def _():
        here = pl.ds(pl.multiple_of(block // 2 * (2 * rows), 2 * rows), 2 * rows)
        copy = pltpu.make_async_copy(w_out_ref.at[0, :, here], columns, sem)
        copy.start()
        copy.wait()
        turned = columns[...].astype(F32).T
        upper = jnp.where(block % 2 == 1, turned[rows:], turned[:rows])
        out_ref[...] = upper.astype(BF16)


def take_shard(which, w_in, w_out, blocks):
    width, hidden = w_in.shape[1], w_in.shape[2]
    rows = width // blocks
    return pl.pallas_call(
        shard_kernel,
        in_specs=[
            pl.BlockSpec(memory_space=pltpu.SMEM),
            pl.BlockSpec(memory_space=pl.ANY),
            pl.BlockSpec(memory_space=pl.ANY),
        ],
        out_specs=_VM(),
        out_shape=jax.ShapeDtypeStruct((rows, hidden), BF16),
        scratch_shapes=[
            pltpu.VMEM((hidden, 2 * rows), BF16),
            pltpu.SemaphoreType.DMA(()),
        ],
        compiler_params=pltpu.CompilerParams(vmem_limit_bytes=FULL),
    )(which, w_in, w_out)


def pick_kernel(tokens_ref, gain_ref, picks_ref, out_ref):
    rows = tokens_ref.shape[0]
    normed = rms_norm(tokens_ref[...].astype(F32), gain_ref[...]).astype(BF16)
    slots = picks_ref.shape[1]
    here = lax.broadcasted_iota(jnp.int32, (rows, slots), 0) == picks_ref[...]
    onehot = jnp.where(here, 1.0, 0.0).astype(BF16)
    out_ref[...] = lax.dot_general(
        onehot, normed, (((0,), (0,)), ((), ())), preferred_element_type=F32
    ).astype(BF16)


def pick_rows(tokens, gain, picks):
    slots, width = picks.shape[1], tokens.shape[1]
    return pl.pallas_call(
        pick_kernel,
        in_specs=[_VM()] * 3,
        out_specs=_VM(),
        out_shape=jax.ShapeDtypeStruct((slots, width), BF16),
        compiler_params=pltpu.CompilerParams(vmem_limit_bytes=VMEM // 4),
    )(tokens, gain, picks)


def gelu(v):
    return 0.5 * v * (1.0 + jnp.tanh(0.7978845608028654 * (v + 0.044715 * (v * v * v))))


def expert_kernel(rows_ref, weights_ref, out_ref, rows_held, w_in, w_out, middle, sems):
    blocks, _, part, hidden = weights_ref.shape
    width = blocks * part
    inner = [pl.ds(i, min(STEP, hidden - i)) for i in range(0, hidden, STEP)]
    outer = [pl.ds(i, STEP // part) for i in range(0, blocks, STEP // part)]
    copies = [
        pltpu.make_async_copy(weights_ref.at[:, 0, :, span], w_in.at[:, :, span], sems.at[n])
        for n, span in enumerate(inner)
    ] + [
        pltpu.make_async_copy(
            weights_ref.at[span, 1], w_out.at[span], sems.at[len(inner) + n]
        )
        for n, span in enumerate(outer)
    ]
    rows_copy = pltpu.make_async_copy(rows_ref, rows_held, sems.at[len(copies)])
    rows_copy.start()
    for copy in copies:
        copy.start()
    rows_copy.wait()
    rows = rows_held[...]
    for n, span in enumerate(inner):
        copies[n].wait()
        first = w_in[:, :, span].reshape(width, -1)
        middle[:, span] = gelu(jnp.dot(rows, first, preferred_element_type=F32)).astype(BF16)
    mid = middle[...]
    for n, span in enumerate(outer):
        copies[len(inner) + n].wait()
        out_ref[:, n * STEP : (n + 1) * STEP] = lax.dot_general(
            mid,
            w_out[span].reshape(STEP, hidden),
            (((1,), (1,)), ((), ())),
            preferred_element_type=F32,
        ).astype(BF16)


def expert(rows, weights):
    total, width = rows.shape
    blocks, _, part, hidden = weights.shape
    return pl.pallas_call(
        expert_kernel,
        in_specs=[pl.BlockSpec(memory_space=pl.ANY)] * 2,
        out_specs=_VM(),
        out_shape=jax.ShapeDtypeStruct((total, width), BF16),
        scratch_shapes=[
            pltpu.VMEM((total, width), BF16),
            pltpu.VMEM((blocks, part, hidden), BF16),
            pltpu.VMEM((blocks, part, hidden), BF16),
            pltpu.VMEM((total, hidden), BF16),
            pltpu.SemaphoreType.DMA((1 + -(-hidden // STEP) + width // STEP,)),
        ],
        compiler_params=pltpu.CompilerParams(vmem_limit_bytes=FULL),
        cost_estimate=pl.CostEstimate(
            flops=4 * total * width * hidden,
            bytes_accessed=4 * width * hidden + 4 * total * width,
            transcendentals=total * hidden,
        ),
    )(rows, weights)


def pieces(v, count):
    out = []
    for _ in range(count):
        part = v.astype(BF16)
        out.append(part)
        v = v - part.astype(F32)
    return out


def tail_kernel(
    back_ref, picks_ref, weight_ref, tokens_ref, gain_ref, joined_ref, query_ref,
    encoded_ref, packet_ref,
):
    rows = tokens_ref.shape[0]
    slots = picks_ref.shape[1]
    here = lax.broadcasted_iota(jnp.int32, (rows, slots), 0) == picks_ref[...]
    spread = jnp.where(here, weight_ref[...], 0.0)
    back = back_ref[...]
    expert_sum = sum(
        jnp.dot(part, back, preferred_element_type=F32) for part in pieces(spread, 3)
    )
    mixed = tokens_ref[...].astype(F32) + expert_sum
    encoded = rms_norm(mixed, gain_ref[...]).astype(BF16)
    encoded_ref[...] = encoded
    joined = jnp.dot(encoded, joined_ref[...], preferred_element_type=F32).astype(BF16)
    keys, values = joined[:, : joined.shape[1] // 2], joined[:, joined.shape[1] // 2 :]
    query = query_ref[...]
    count, features = query.shape
    size = features // HEADS
    lane = lax.broadcasted_iota(jnp.int32, (rows, 2 * size), 1)
    low = lane < size
    zero = jnp.zeros((), BF16)
    stat_lane = lax.broadcasted_iota(jnp.int32, (count, 128), 1)
    stats = jnp.zeros((count, 128), F32)
    for pair in range(HEADS // 2):
        span = slice(pair * 2 * size, (pair + 1) * 2 * size)
        q, k, v = query[:, span], keys[:, span], values[:, span]
        total = None
        for odd in range(2):
            mask = low if odd == 0 else ~low
            scores = lax.dot_general(
                q,
                jnp.where(mask, k, zero),
                (((1,), (1,)), ((), ())),
                preferred_element_type=F32,
            ) * (size**-0.5)
            top = jnp.max(scores, axis=1, keepdims=True)
            weights = jnp.exp(scores - top)
            amount = jnp.sum(weights, axis=1, keepdims=True)
            term = jnp.dot(
                weights.astype(BF16), jnp.where(mask, v, zero), preferred_element_type=F32
            )
            total = term if total is None else total + term
            entries = pieces(top, 3) + pieces(amount, 2)
            for i, entry in enumerate(entries):
                at = (2 * pair + odd) * STATS + i
                stats = jnp.where(stat_lane == at, entry.astype(F32), stats)
        packet_ref[:, span] = total.astype(BF16)
    packet_ref[:, features:] = stats.astype(BF16)


def tail(back, picks, weight, tokens, gain, joined, query):
    rows, width = tokens.shape
    count, features = query.shape
    return pl.pallas_call(
        tail_kernel,
        in_specs=[_VM()] * 7,
        out_specs=(_VM(), _VM()),
        out_shape=(
            jax.ShapeDtypeStruct((rows, width), BF16),
            jax.ShapeDtypeStruct((count, features + 128), BF16),
        ),
        compiler_params=pltpu.CompilerParams(vmem_limit_bytes=VMEM // 2),
    )(back, picks, weight, tokens, gain, joined, query)


def merge_kernel(got_ref, proj_ref, out_ref):
    group, count, wide = got_ref.shape
    features = wide - 128
    size = features // HEADS
    lane = lax.broadcasted_iota(jnp.int32, (count, 2 * size), 1)
    low = lane < size
    stats = [got_ref[g, :, features:].astype(F32) for g in range(group)]
    parts = []
    for pair in range(HEADS // 2):
        span = slice(pair * 2 * size, (pair + 1) * 2 * size)
        scales, totals = [], []
        for odd in range(2):
            at = (2 * pair + odd) * STATS
            tops = [s[:, at : at + 1] + s[:, at + 1 : at + 2] + s[:, at + 2 : at + 3] for s in stats]
            amounts = [s[:, at + 3 : at + 4] + s[:, at + 4 : at + 5] for s in stats]
            top = functools.reduce(jnp.maximum, tops)
            scale = [jnp.exp(t - top) for t in tops]
            scales.append(scale)
            totals.append(sum(a * s for a, s in zip(amounts, scale)))
        weighted = sum(
            got_ref[g, :, span].astype(F32) * jnp.where(low, scales[0][g], scales[1][g])
            for g in range(group)
        )
        parts.append((weighted / jnp.where(low, totals[0], totals[1])).astype(BF16))
    context = jnp.concatenate(parts, axis=1)
    out_ref[...] = jnp.dot(context, proj_ref[...], preferred_element_type=F32).astype(BF16)


def merge(got, w_proj):
    return pl.pallas_call(
        merge_kernel,
        in_specs=[_VM()] * 2,
        out_specs=_VM(),
        out_shape=jax.ShapeDtypeStruct((got.shape[1], w_proj.shape[1]), BF16),
        compiler_params=pltpu.CompilerParams(vmem_limit_bytes=VMEM // 4),
    )(got, w_proj)


def scatter_pairs(sizes):
    dps, blocks, parities, rows, cores = sizes
    plane = dps * rows * cores

    def place(dp, z, row, core):
        return ((dp * blocks * parities + z) * rows + row) * cores + core

    pairs = []
    for dp in range(dps):
        for parity in range(parities):
            for row in range(rows):
                e = (dp * parities + parity) * rows + row
                for block in range(blocks):
                    for core in range(cores):
                        j = block * cores + core
                        column = (STEP_J * j + STEP_E * e) % plane
                        source = place(
                            column // (rows * cores), e, column // cores % rows, column % cores
                        )
                        pairs.append((source, place(dp, block * parities + parity, row, core)))
    return pairs


def local(
    sizes, tokens, picks, gates, counts, norm_in, norm_out, w_in, w_out, w_key, w_value, queries, w_proj
):
    dps, blocks, parities, row_count, cores = sizes
    plane = dps * row_count * cores
    experts, cap = picks.shape[1], picks.shape[2]
    width = tokens.shape[1]
    own = lax.axis_index("block") * parities + lax.axis_index("parity")
    column = (lax.axis_index("dp") * row_count + lax.axis_index("row")) * cores + lax.axis_index(
        "core"
    )
    j = (INV_J * (column + (plane - STEP_E) * own)) % plane
    shard = take_shard(jnp.stack([j // cores, j % cores]).astype(jnp.int32), w_in, w_out, blocks)
    shard = lax.ppermute(shard, ALL, scatter_pairs(sizes))
    query = lax.all_gather(queries, SEQ, tiled=True)
    shard, query = lax.optimization_barrier((shard, query))
    weights = lax.all_gather(shard, ("block", "core"))
    weights = weights.reshape(blocks, cores, *shard.shape)

    pick_row = picks.reshape(1, experts * cap)
    live = lax.broadcasted_iota(jnp.int32, (experts, cap), 1) < counts[0][:, None]
    slot_weight = jnp.where(live, gates[0], 0.0).reshape(1, experts * cap)
    chosen = pick_rows(tokens, norm_in[None, :], pick_row)
    there = lax.all_to_all(
        chosen.reshape(experts, -1, width), NEAR, split_axis=0, concat_axis=0, tiled=True
    )
    joined = jnp.concatenate([w_key, w_value], axis=1)
    there, joined, slot_weight = lax.optimization_barrier((there, joined, slot_weight))
    result = expert(there.reshape(-1, width), weights)
    back = lax.all_to_all(
        result.reshape(experts, -1, width), NEAR, split_axis=0, concat_axis=0, tiled=True
    ).reshape(-1, width)
    encoded, packet = tail(
        back, pick_row, slot_weight, tokens, norm_out[None, :], joined, query
    )
    group = row_count * cores
    got = lax.all_to_all(
        packet.reshape(group, -1, packet.shape[1]), SEQ, split_axis=0, concat_axis=0, tiled=True
    )
    return encoded, merge(got, w_proj)


def solution(mesh):
    dps, planes, seq = mesh.shape["dp"], mesh.shape["expert"], mesh.shape["seq"]
    sizes = (dps, planes // BLOCK, BLOCK, seq // 2, 2)
    split = Mesh(mesh.devices.reshape(sizes), ALL)
    in_specs = (
        P(ALL, None),
        P(ALL, None, None),
        P(ALL, None, None),
        P(ALL, None),
        P(),
        P(),
        P(("block", "parity"), None, None),
        P(("block", "parity"), None, None),
        P(),
        P(),
        P(ALL, None),
        P(),
    )
    out_specs = (P(ALL, None), P(ALL, None))
    return jax.shard_map(
        functools.partial(local, sizes),
        mesh=split,
        in_specs=in_specs,
        out_specs=out_specs,
        check_vma=False,
    )
```

```python
import functools

import jax
import jax.numpy as jnp
from jax import lax
from jax.experimental import pallas as pl
from jax.experimental.pallas import tpu as pltpu
from jax.sharding import Mesh
from jax.sharding import PartitionSpec as P

HEADS = 8
EPSILON = 1e-06
BLOCK = 2
ALL = ("dp", "block", "parity", "row", "core")
NEAR = ("dp", "parity", "row")
SEQ = ("row", "core")
STEP_J, STEP_E, INV_J = 9, 30, 25
STATS = 5
STEP = 512
VMEM = 60 * 1024 * 1024
FULL = 61 * 1024 * 1024
F32 = jnp.float32
BF16 = jnp.bfloat16

_VM = functools.partial(pl.BlockSpec, memory_space=pltpu.VMEM)


def rms_norm(values, gain):
    mean_square = jnp.mean(values * values, axis=-1, keepdims=True)
    return values * lax.rsqrt(mean_square + EPSILON) * gain


def shard_kernel(which, w_in_ref, w_out_ref, out_ref, columns, sem):
    rows = out_ref.shape[0]
    block, kind = which[0], which[1]

    @pl.when(kind == 0)
    def _():
        here = pl.ds(pl.multiple_of(block * rows, rows), rows)
        copy = pltpu.make_async_copy(w_in_ref.at[0, here, :], out_ref, sem)
        copy.start()
        copy.wait()

    @pl.when(kind == 1)
    def _():
        here = pl.ds(pl.multiple_of(block // 2 * (2 * rows), 2 * rows), 2 * rows)
        copy = pltpu.make_async_copy(w_out_ref.at[0, :, here], columns, sem)
        copy.start()
        copy.wait()
        turned = columns[...].astype(F32).T
        upper = jnp.where(block % 2 == 1, turned[rows:], turned[:rows])
        out_ref[...] = upper.astype(BF16)


def take_shard(which, w_in, w_out, blocks):
    width, hidden = w_in.shape[1], w_in.shape[2]
    rows = width // blocks
    return pl.pallas_call(
        shard_kernel,
        in_specs=[
            pl.BlockSpec(memory_space=pltpu.SMEM),
            pl.BlockSpec(memory_space=pl.ANY),
            pl.BlockSpec(memory_space=pl.ANY),
        ],
        out_specs=_VM(),
        out_shape=jax.ShapeDtypeStruct((rows, hidden), BF16),
        scratch_shapes=[
            pltpu.VMEM((hidden, 2 * rows), BF16),
            pltpu.SemaphoreType.DMA(()),
        ],
        compiler_params=pltpu.CompilerParams(vmem_limit_bytes=FULL),
    )(which, w_in, w_out)


def pick_kernel(tokens_ref, gain_ref, picks_ref, out_ref):
    rows = tokens_ref.shape[0]
    normed = rms_norm(tokens_ref[...].astype(F32), gain_ref[...]).astype(BF16)
    slots = picks_ref.shape[1]
    here = lax.broadcasted_iota(jnp.int32, (rows, slots), 0) == picks_ref[...]
    onehot = jnp.where(here, 1.0, 0.0).astype(BF16)
    out_ref[...] = lax.dot_general(
        onehot, normed, (((0,), (0,)), ((), ())), preferred_element_type=F32
    ).astype(BF16)


def pick_rows(tokens, gain, picks):
    slots, width = picks.shape[1], tokens.shape[1]
    return pl.pallas_call(
        pick_kernel,
        in_specs=[_VM()] * 3,
        out_specs=_VM(),
        out_shape=jax.ShapeDtypeStruct((slots, width), BF16),
        compiler_params=pltpu.CompilerParams(vmem_limit_bytes=VMEM // 4),
    )(tokens, gain, picks)


def gelu(v):
    return 0.5 * v * (1.0 + jnp.tanh(0.7978845608028654 * (v + 0.044715 * (v * v * v))))


def expert_kernel(rows_ref, weights_ref, out_ref, rows_held, w_in, w_out, middle, sems):
    blocks, _, part, hidden = weights_ref.shape
    width = blocks * part
    inner = [pl.ds(i, min(STEP, hidden - i)) for i in range(0, hidden, STEP)]
    outer = [pl.ds(i, STEP // part) for i in range(0, blocks, STEP // part)]
    copies = [
        pltpu.make_async_copy(weights_ref.at[:, 0, :, span], w_in.at[:, :, span], sems.at[n])
        for n, span in enumerate(inner)
    ] + [
        pltpu.make_async_copy(
            weights_ref.at[span, 1], w_out.at[span], sems.at[len(inner) + n]
        )
        for n, span in enumerate(outer)
    ]
    rows_copy = pltpu.make_async_copy(rows_ref, rows_held, sems.at[len(copies)])
    rows_copy.start()
    for copy in copies:
        copy.start()
    rows_copy.wait()
    rows = rows_held[...]
    for n, span in enumerate(inner):
        copies[n].wait()
        first = w_in[:, :, span].reshape(width, -1)
        middle[:, span] = gelu(jnp.dot(rows, first, preferred_element_type=F32)).astype(BF16)
    mid = middle[...]
    for n, span in enumerate(outer):
        copies[len(inner) + n].wait()
        out_ref[:, n * STEP : (n + 1) * STEP] = lax.dot_general(
            mid,
            w_out[span].reshape(STEP, hidden),
            (((1,), (1,)), ((), ())),
            preferred_element_type=F32,
        ).astype(BF16)


def expert(rows, weights):
    total, width = rows.shape
    blocks, _, part, hidden = weights.shape
    return pl.pallas_call(
        expert_kernel,
        in_specs=[pl.BlockSpec(memory_space=pl.ANY)] * 2,
        out_specs=_VM(),
        out_shape=jax.ShapeDtypeStruct((total, width), BF16),
        scratch_shapes=[
            pltpu.VMEM((total, width), BF16),
            pltpu.VMEM((blocks, part, hidden), BF16),
            pltpu.VMEM((blocks, part, hidden), BF16),
            pltpu.VMEM((total, hidden), BF16),
            pltpu.SemaphoreType.DMA((1 + -(-hidden // STEP) + width // STEP,)),
        ],
        compiler_params=pltpu.CompilerParams(vmem_limit_bytes=FULL),
        cost_estimate=pl.CostEstimate(
            flops=4 * total * width * hidden,
            bytes_accessed=4 * width * hidden + 4 * total * width,
            transcendentals=total * hidden,
        ),
    )(rows, weights)


def pieces(v, count):
    out = []
    for _ in range(count):
        part = v.astype(BF16)
        out.append(part)
        v = v - part.astype(F32)
    return out


def tail_kernel(
    back_ref, picks_ref, weight_ref, tokens_ref, gain_ref, joined_ref, query_ref,
    encoded_ref, packet_ref,
):
    rows = tokens_ref.shape[0]
    slots = picks_ref.shape[1]
    here = lax.broadcasted_iota(jnp.int32, (rows, slots), 0) == picks_ref[...]
    spread = jnp.where(here, weight_ref[...], 0.0)
    back = back_ref[...]
    expert_sum = sum(
        jnp.dot(part, back, preferred_element_type=F32) for part in pieces(spread, 3)
    )
    mixed = tokens_ref[...].astype(F32) + expert_sum
    encoded = rms_norm(mixed, gain_ref[...]).astype(BF16)
    encoded_ref[...] = encoded
    joined = jnp.dot(encoded, joined_ref[...], preferred_element_type=F32).astype(BF16)
    keys, values = joined[:, : joined.shape[1] // 2], joined[:, joined.shape[1] // 2 :]
    query = query_ref[...]
    count, features = query.shape
    size = features // HEADS
    lane = lax.broadcasted_iota(jnp.int32, (rows, 2 * size), 1)
    low = lane < size
    zero = jnp.zeros((), BF16)
    stat_lane = lax.broadcasted_iota(jnp.int32, (count, 128), 1)
    stats = jnp.zeros((count, 128), F32)
    for pair in range(HEADS // 2):
        span = slice(pair * 2 * size, (pair + 1) * 2 * size)
        q, k, v = query[:, span], keys[:, span], values[:, span]
        total = None
        for odd in range(2):
            mask = low if odd == 0 else ~low
            scores = lax.dot_general(
                q,
                jnp.where(mask, k, zero),
                (((1,), (1,)), ((), ())),
                preferred_element_type=F32,
            ) * (size**-0.5)
            top = jnp.max(scores, axis=1, keepdims=True)
            weights = jnp.exp(scores - top)
            amount = jnp.sum(weights, axis=1, keepdims=True)
            term = jnp.dot(
                weights.astype(BF16), jnp.where(mask, v, zero), preferred_element_type=F32
            )
            total = term if total is None else total + term
            entries = pieces(top, 3) + pieces(amount, 2)
            for i, entry in enumerate(entries):
                at = (2 * pair + odd) * STATS + i
                stats = jnp.where(stat_lane == at, entry.astype(F32), stats)
        packet_ref[:, span] = total.astype(BF16)
    packet_ref[:, features:] = stats.astype(BF16)


def tail(back, picks, weight, tokens, gain, joined, query):
    rows, width = tokens.shape
    count, features = query.shape
    return pl.pallas_call(
        tail_kernel,
        in_specs=[_VM()] * 7,
        out_specs=(_VM(), _VM()),
        out_shape=(
            jax.ShapeDtypeStruct((rows, width), BF16),
            jax.ShapeDtypeStruct((count, features + 128), BF16),
        ),
        compiler_params=pltpu.CompilerParams(vmem_limit_bytes=VMEM // 2),
    )(back, picks, weight, tokens, gain, joined, query)


def merge_kernel(got_ref, proj_ref, out_ref):
    group, count, wide = got_ref.shape
    features = wide - 128
    size = features // HEADS
    lane = lax.broadcasted_iota(jnp.int32, (count, 2 * size), 1)
    low = lane < size
    stats = [got_ref[g, :, features:].astype(F32) for g in range(group)]
    parts = []
    for pair in range(HEADS // 2):
        span = slice(pair * 2 * size, (pair + 1) * 2 * size)
        scales, totals = [], []
        for odd in range(2):
            at = (2 * pair + odd) * STATS
            tops = [s[:, at : at + 1] + s[:, at + 1 : at + 2] + s[:, at + 2 : at + 3] for s in stats]
            amounts = [s[:, at + 3 : at + 4] + s[:, at + 4 : at + 5] for s in stats]
            top = functools.reduce(jnp.maximum, tops)
            scale = [jnp.exp(t - top) for t in tops]
            scales.append(scale)
            totals.append(sum(a * s for a, s in zip(amounts, scale)))
        weighted = sum(
            got_ref[g, :, span].astype(F32) * jnp.where(low, scales[0][g], scales[1][g])
            for g in range(group)
        )
        parts.append((weighted / jnp.where(low, totals[0], totals[1])).astype(BF16))
    context = jnp.concatenate(parts, axis=1)
    out_ref[...] = jnp.dot(context, proj_ref[...], preferred_element_type=F32).astype(BF16)


def merge(got, w_proj):
    return pl.pallas_call(
        merge_kernel,
        in_specs=[_VM()] * 2,
        out_specs=_VM(),
        out_shape=jax.ShapeDtypeStruct((got.shape[1], w_proj.shape[1]), BF16),
        compiler_params=pltpu.CompilerParams(vmem_limit_bytes=VMEM // 4),
    )(got, w_proj)


def scatter_pairs(sizes):
    dps, blocks, parities, rows, cores = sizes
    plane = dps * rows * cores

    def place(dp, z, row, core):
        return ((dp * blocks * parities + z) * rows + row) * cores + core

    pairs = []
    for dp in range(dps):
        for parity in range(parities):
            for row in range(rows):
                e = (dp * parities + parity) * rows + row
                for block in range(blocks):
                    for core in range(cores):
                        j = block * cores + core
                        column = (STEP_J * j + STEP_E * e) % plane
                        source = place(
                            column // (rows * cores), e, column // cores % rows, column % cores
                        )
                        pairs.append((source, place(dp, block * parities + parity, row, core)))
    return pairs


def local(
    sizes, tokens, picks, gates, counts, norm_in, norm_out, w_in, w_out, w_key, w_value, queries, w_proj
):
    dps, blocks, parities, row_count, cores = sizes
    plane = dps * row_count * cores
    experts, cap = picks.shape[1], picks.shape[2]
    width = tokens.shape[1]
    own = lax.axis_index("block") * parities + lax.axis_index("parity")
    column = (lax.axis_index("dp") * row_count + lax.axis_index("row")) * cores + lax.axis_index(
        "core"
    )
    j = (INV_J * (column + (plane - STEP_E) * own)) % plane
    shard = take_shard(jnp.stack([j // cores, j % cores]).astype(jnp.int32), w_in, w_out, blocks)
    shard = lax.ppermute(shard, ALL, scatter_pairs(sizes))
    shard, queries = lax.optimization_barrier((shard, queries))
    query = lax.all_gather(queries, SEQ, tiled=True)
    weights = lax.all_gather(shard, ("block", "core"))
    weights = weights.reshape(blocks, cores, *shard.shape)

    pick_row = picks.reshape(1, experts * cap)
    live = lax.broadcasted_iota(jnp.int32, (experts, cap), 1) < counts[0][:, None]
    slot_weight = jnp.where(live, gates[0], 0.0).reshape(1, experts * cap)
    chosen = pick_rows(tokens, norm_in[None, :], pick_row)
    there = lax.all_to_all(
        chosen.reshape(experts, -1, width), NEAR, split_axis=0, concat_axis=0, tiled=True
    )
    joined = jnp.concatenate([w_key, w_value], axis=1)
    there, joined, slot_weight, query = lax.optimization_barrier(
        (there, joined, slot_weight, query)
    )
    result = expert(there.reshape(-1, width), weights)
    back = lax.all_to_all(
        result.reshape(experts, -1, width), NEAR, split_axis=0, concat_axis=0, tiled=True
    ).reshape(-1, width)
    encoded, packet = tail(
        back, pick_row, slot_weight, tokens, norm_out[None, :], joined, query
    )
    group = row_count * cores
    got = lax.all_to_all(
        packet.reshape(group, -1, packet.shape[1]), SEQ, split_axis=0, concat_axis=0, tiled=True
    )
    return encoded, merge(got, w_proj)


def solution(mesh):
    dps, planes, seq = mesh.shape["dp"], mesh.shape["expert"], mesh.shape["seq"]
    sizes = (dps, planes // BLOCK, BLOCK, seq // 2, 2)
    split = Mesh(mesh.devices.reshape(sizes), ALL)
    in_specs = (
        P(ALL, None),
        P(ALL, None, None),
        P(ALL, None, None),
        P(ALL, None),
        P(),
        P(),
        P(("block", "parity"), None, None),
        P(("block", "parity"), None, None),
        P(),
        P(),
        P(ALL, None),
        P(),
    )
    out_specs = (P(ALL, None), P(ALL, None))
    return jax.shard_map(
        functools.partial(local, sizes),
        mesh=split,
        in_specs=in_specs,
        out_specs=out_specs,
        check_vma=False,
    )
```
